32 devices in a mesh: sky: 8 (over y, x, core), visit: 4 (over z).
Axes of the slice: x: 2, y: 2, z: 4, core: 2. Of those that a mesh axis runs over, the one named last changes fastest.
Arguments:
- images: bfloat16 [32, 768, 2048], P('visit', 'sky'), may hold values from -6 to 6
- inv_var: bfloat16 [32, 768, 2048], P('visit', 'sky'), may hold values from 0.25 to 4
- row_taps: bfloat16 [11, 41], replicated, may hold values from -1 to 1
- col_taps: bfloat16 [11, 41], replicated, may hold values from -1 to 1
- coeffs: float32 [32, 11, 3], replicated, may hold values from -4 to 4
- dithers: int32 [32], replicated, may hold values from 0 to 256, as said below
- depths: int32 [8], P('sky'), may hold values from 2 to 16, as said below
Outputs:
- coadd: float32 [768, 2048], P('sky', 'visit')
The draws below stay inside these ranges and needn't reach their ends.
Inputs may be any that keep to these rules, and one draw needn't show every extreme that they name: `dithers`: some visit has offset 0 and some has offset 256. `depths`: some tile is covered by 16 visits.
All inputs are finite; a program needn't handle non-finite values.
Results may differ from the reference program's by a relative error of at most 0.0029.
Values may be sent and summed in bfloat16 or wider, within the bound.
A program may use at most 64 MiB of HBM per device.

```python
import math
import jax
import jax.numpy as jnp
from jax import lax

ROWS = 96
NX = 2048
VISITS = 32
NB = 11
TAPS = 41
DEPTH_MAX = 16
DITHER = 256
TILES = 8
NY = 768


def draw_dithers(key, part):
    drawn_vals = jax.random.randint(key, (VISITS,), 0, DITHER + 1)
    shuffled = jax.random.permutation(jax.random.fold_in(key, 5), VISITS)
    return drawn_vals.at[shuffled[0]].set(0).at[shuffled[1]].set(DITHER).astype(jnp.int32)


def draw_depths(key, part):
    drawn_vals = jax.random.randint(key, (TILES,), 0, DEPTH_MAX - 1)
    depth_vals = 2 + drawn_vals * drawn_vals // (DEPTH_MAX - 2)
    chosen = jax.random.randint(jax.random.fold_in(key, 11), (), 0, TILES)
    return depth_vals.at[chosen].set(DEPTH_MAX).astype(jnp.int32)


def levels(key, shape, split, least, top_value):
    factor_of, own = 1.0, jax.random.fold_in(key, 6)
    for axis_at, shards_of in split:
        draws = jnp.exp(jax.random.uniform(jax.random.fold_in(own, axis_at), (shards_of,), jnp.float32, least / len(split), top_value / len(split)))
        factor_of = factor_of * jnp.repeat(draws, shape[axis_at] // shards_of).reshape([-1 if axis == axis_at else 1 for axis in range(len(shape))])
    return factor_of


def normal_values(stream_key, extent, deviation, limit, shards=(), held_as=jnp.bfloat16):
    array = jax.random.normal(stream_key, extent, jnp.float32) * deviation
    if len(shards) > 0:
        array = levels(stream_key, extent, shards, -0.22, 0.18) * array
    return jnp.clip(array, min=-limit, max=limit).astype(held_as)


def setup_inputs(seed: int = 0) -> dict:
    key_list = jax.random.split(jax.random.key(seed), 8)
    images = normal_values(key_list[0], (VISITS, NY, NX), 1.0, 6.0, ((0, 4), (1, 8)))
    inv_var = jnp.clip(jnp.exp(math.log(4.0) - 2.7725887 * jax.random.uniform(key_list[1], (VISITS, NY, NX), jnp.float32) ** levels(key_list[1], (VISITS, NY, NX), ((0, 4), (1, 8)), -0.2, 0.2)), 0.25, 4.0).astype(jnp.bfloat16)
    row_taps = normal_values(key_list[2], (NB, TAPS), TAPS ** -0.5, 1.0)
    col_taps = normal_values(key_list[3], (NB, TAPS), TAPS ** -0.5, 1.0)
    coeffs = normal_values(key_list[4], (VISITS, NB, 3), 0.3, 4.0, (), jnp.float32)
    dithers = draw_dithers(jax.random.fold_in(key_list[7], 71), 0)
    depths = draw_depths(jax.random.fold_in(key_list[7], 71), 0)
    return {"images": images, "inv_var": inv_var, "row_taps": row_taps, "col_taps": col_taps, "coeffs": coeffs, "dithers": dithers, "depths": depths}


def reference(images, inv_var, row_taps, col_taps, coeffs, dithers, depths):
    half_taps = TAPS // 2
    row_kernel = row_taps.astype(jnp.float32)[:, None, :, None]
    col_kernel = col_taps.astype(jnp.float32)[:, None, None, :]
    col_ids = jnp.arange(NX, dtype=jnp.int32)
    row_ids = jnp.arange(NY, dtype=jnp.int32)
    col_coord = (2.0 * col_ids.astype(jnp.float32) + 1.0) / NX - 1.0
    row_coord = (2.0 * row_ids.astype(jnp.float32) + 1.0) / NY - 1.0
    tile_row = row_ids // ROWS
    first_visit = (tile_row * VISITS // TILES).astype(jnp.int32)
    row_depth = depths[tile_row]

    def one_visit(carry, visit):
        numerator, denominator = carry
        visit_plane = images[visit].astype(jnp.float32)[None, None]
        passed = lax.conv_general_dilated(visit_plane, row_kernel, (1, 1), ((half_taps, half_taps), (0, 0)), dimension_numbers=("NCHW", "OIHW", "NCHW"), precision=lax.Precision.HIGHEST)
        passed = lax.optimization_barrier(passed.astype(jnp.bfloat16)).astype(jnp.float32)
        basis_image = lax.conv_general_dilated(passed, col_kernel, (1, 1), ((0, 0), (half_taps, half_taps)), dimension_numbers=("NCHW", "OIHW", "NCHW"), feature_group_count=NB, precision=lax.Precision.HIGHEST)[0]
        coef_rows = coeffs[visit]
        spatial = coef_rows[:, 0, None, None] + coef_rows[:, 1, None, None] * col_coord[None, None, :] + coef_rows[:, 2, None, None] * row_coord[None, :, None]
        matched = jnp.sum(spatial * basis_image, axis=0)
        shift_cols = dithers[visit]
        inside = (col_ids >= shift_cols) & (col_ids < shift_cols + NX - DITHER)
        covered = jnp.mod(visit - first_visit, VISITS) < row_depth
        weight = inv_var[visit].astype(jnp.float32) * inside.astype(jnp.float32)[None, :] * covered.astype(jnp.float32)[:, None]
        return (numerator + weight * matched, denominator + weight), None

    starting = (jnp.zeros((NY, NX), jnp.float32), jnp.zeros((NY, NX), jnp.float32))
    (numerator, denominator), _ = lax.scan(one_visit, starting, jnp.arange(VISITS, dtype=jnp.int32))
    return numerator / (1.0 + denominator)
```

```python
import jax
import jax.numpy as jnp
from jax import lax
from jax.experimental import pallas as pl
from jax.experimental.pallas import tpu as pltpu
from jax.sharding import PartitionSpec as P

DITHER = 256
DEPTH_MAX = 16
WIN = 256
PAIR = 2


def row_tables(taps, rows, depth):
    count = taps.shape[1]
    half = count // 2
    spot = jnp.arange(depth, dtype=jnp.int32)
    rel = jnp.where(
        spot < rows,
        spot,
        jnp.where(spot < rows + half, spot - rows - half, spot - half),
    )
    rel = jnp.where(spot < rows + 2 * half, rel, -4 * rows)
    offsets = rel[None, :] - jnp.arange(rows, dtype=jnp.int32)[:, None] + half
    picks = (offsets[None] == jnp.arange(count, dtype=jnp.int32)[:, None, None]).astype(jnp.bfloat16)
    table = jnp.einsum("kt,toi->koi", taps, picks, preferred_element_type=jnp.float32)
    return table.astype(jnp.bfloat16).reshape(-1, depth)


def col_tables(taps, step):
    count = taps.shape[1]
    spot = jnp.arange(WIN, dtype=jnp.int32)
    offsets = jnp.where(spot[None, :] < step, spot[:, None] - spot[None, :], -1)
    picks = (offsets[None] == jnp.arange(count, dtype=jnp.int32)[:, None, None]).astype(jnp.bfloat16)
    table = jnp.einsum("kt,tio->kio", taps, picks, preferred_element_type=jnp.float32)
    return table.astype(jnp.bfloat16)


def coadd_kernel(
    sizes, coef_ref, shift_ref, cover_ref, first_ref, img_ref, inv_ref, row_ref, col_ref,
    num_ref, den_ref, pass_ref,
):
    visits, rows, cols, total_rows, step = sizes
    basis = col_ref.shape[0]
    pairs = img_ref.shape[1] // PAIR
    num_ref[...] = jnp.zeros_like(num_ref)
    den_ref[...] = jnp.zeros_like(den_ref)
    row_ids = first_ref[0] + lax.broadcasted_iota(jnp.int32, (rows, 128), 0)
    row_coord = (2.0 * row_ids.astype(jnp.float32) + 1.0) / total_rows - 1.0
    row_coord = jnp.concatenate([row_coord] * (WIN // 128), axis=1)[None]
    lane = lax.broadcasted_iota(jnp.int32, (PAIR, 1, WIN), 2)
    place = lax.broadcasted_iota(jnp.int32, (PAIR, 1, WIN), 0)

    def one_visit(v, carry):
        @pl.when(cover_ref[v] != 0)
        def _():
            shift = shift_ref[v]

            def one_pair(q, inner):
                col_ids = (q * PAIR + place) * step + lane
                col_coord = (2.0 * col_ids.astype(jnp.float32) + 1.0) / cols - 1.0
                for j in range(PAIR):
                    passed = jnp.dot(
                        row_ref[...], img_ref[v, q * PAIR + j], preferred_element_type=jnp.float32
                    )
                    pass_ref[:, j] = passed.astype(jnp.bfloat16).reshape(basis, rows, WIN)
                matched = jnp.zeros((PAIR, rows, WIN), jnp.float32)
                for k in range(basis):
                    image = jnp.dot(
                        pass_ref[k].reshape(PAIR * rows, WIN),
                        col_ref[k],
                        preferred_element_type=jnp.float32,
                    ).reshape(PAIR, rows, WIN)
                    c0 = coef_ref[v, 3 * k]
                    c1 = coef_ref[v, 3 * k + 1]
                    c2 = coef_ref[v, 3 * k + 2]
                    spatial = (c0 + c1 * col_coord) + c2 * row_coord
                    matched = matched + spatial * image
                inside = (col_ids >= shift) & (col_ids < shift + cols - DITHER)
                where_ok = jnp.broadcast_to(inside, (PAIR, rows, WIN))
                at = pl.ds(q * PAIR, PAIR)
                weight = jnp.where(where_ok, inv_ref[v, at].astype(jnp.float32), 0.0)
                num_ref[at] += weight * matched
                den_ref[at] += weight
                return inner

            lax.fori_loop(0, pairs, one_pair, 0)

        return carry

    lax.fori_loop(0, visits, one_visit, 0)


def local(images, inv_var, row_taps, col_taps, coeffs, dithers, depths):
    visit_count, row_count, col_count = images.shape
    basis, taps = row_taps.shape
    half = taps // 2
    sky = lax.axis_index("sky")
    tiles = lax.axis_size("sky")
    group = lax.axis_index("visit")
    groups = lax.axis_size("visit")
    visits_all = visit_count * groups
    total_rows = row_count * tiles
    step = WIN - 2 * half
    wins = -(-col_count // step)
    wins = -(-wins // PAIR) * PAIR
    depth = -(-(row_count + 2 * half) // 16) * 16

    up = lax.ppermute(
        images[:, row_count - half :], "sky", [(i, i + 1) for i in range(tiles - 1)]
    )
    down = lax.ppermute(images[:, :half], "sky", [(i + 1, i) for i in range(tiles - 1)])
    row_table = row_tables(row_taps, row_count, depth)
    col_table = col_tables(col_taps, step)
    tall = jnp.concatenate([images, up, down], axis=1)
    span = (wins - 1) * step + WIN
    tall = jnp.pad(
        tall,
        ((0, 0), (0, depth - row_count - 2 * half), (half, span - half - col_count)),
    )
    img_win = jnp.stack([tall[:, :, w * step : w * step + WIN] for w in range(wins)], axis=1)
    inv_pad = jnp.pad(inv_var, ((0, 0), (0, 0), (0, span - col_count)))
    inv_win = jnp.stack([inv_pad[:, :, w * step : w * step + WIN] for w in range(wins)], axis=1)

    order = group * visit_count + jnp.arange(visit_count, dtype=jnp.int32)
    first_visit = sky * visits_all // tiles
    covered = (jnp.mod(order - first_visit, visits_all) < depths[0]).astype(jnp.int32)
    coef = lax.dynamic_slice_in_dim(coeffs, group * visit_count, visit_count, 0)
    coef = coef.reshape(visit_count, basis * 3)
    shifts = lax.dynamic_slice_in_dim(dithers, group * visit_count, visit_count, 0)
    first_row = (sky * row_count).astype(jnp.int32).reshape(1)

    smem = pl.BlockSpec(memory_space=pltpu.SMEM)
    vmem = pl.BlockSpec(memory_space=pltpu.VMEM)
    out = jax.ShapeDtypeStruct((wins, row_count, WIN), jnp.float32)
    sizes = (visit_count, row_count, col_count, total_rows, step)

    def body(*refs):
        coadd_kernel(sizes, *refs)

    num, den = pl.pallas_call(
        body,
        out_shape=(out, out),
        in_specs=[smem] * 4 + [vmem] * 4,
        out_specs=(vmem, vmem),
        scratch_shapes=[pltpu.VMEM((basis, PAIR, row_count, WIN), jnp.bfloat16)],
        compiler_params=pltpu.CompilerParams(vmem_limit_bytes=48 * 1024 * 1024),
    )(coef, shifts, covered, first_row, img_win, inv_win, row_table, col_table)

    def flat(x):
        return jnp.concatenate([x[w, :, :step] for w in range(wins)], axis=1)[:, :col_count]

    both = jnp.stack([flat(num), flat(den)], axis=0)
    both = lax.psum_scatter(both, "visit", scatter_dimension=2, tiled=True)
    return both[0] / (1.0 + both[1])


def solution(mesh):
    placed = (P("visit", "sky", None), P("visit", "sky", None), P(), P(), P(), P(), P("sky"))
    return jax.shard_map(
        local, mesh=mesh, in_specs=placed, out_specs=P("sky", "visit"), check_vma=False
    )
```

```python
import jax
import jax.numpy as jnp
from jax import lax
from jax.experimental import pallas as pl
from jax.experimental.pallas import tpu as pltpu
from jax.sharding import PartitionSpec as P

DITHER = 256
DEPTH_MAX = 16
WIN = 256
PAIR = 2
LANE = 128
EDGE = 32
MESH = pl.DeviceIdType.MESH


def base_rows(row_taps, col_taps, rows):
    basis, taps = row_taps.shape
    half = taps // 2
    spot = jnp.arange(WIN, dtype=jnp.int32)

    def placed(table, which):
        picks = which[None, :] == jnp.arange(taps, dtype=jnp.int32)[:, None]
        return jnp.sum(
            jnp.where(picks[None], table.astype(jnp.float32)[:, :, None], 0.0), axis=1
        )

    own = placed(row_taps, jnp.mod(spot + half, WIN))
    above = placed(row_taps, spot - (LANE + EDGE - half))
    across = placed(col_taps, jnp.mod(-spot, WIN))
    return jnp.stack([own, above, across], axis=1)


def kernel(
    sizes,
    coef_ref, shift_ref, depth_ref, base_ref, img_ref, inv_ref,
    out_ref,
    buf, inv, row_tab, col_tab, passed, acc, flat, outgo, income,
    img_sem, inv_sem, halo_send, halo_recv, part_send, part_recv,
):
    tiles, groups, step = sizes
    visits, rows, cols = img_ref.shape
    basis = base_ref.shape[0]
    visits_all = visits * groups
    total_rows = rows * tiles
    strip = cols // groups
    width = buf.shape[2]
    deep = rows + 2 * EDGE
    pairs = groups + 1
    body = pl.ds(LANE, cols)

    t = lax.axis_index("sky")
    g = lax.axis_index("visit")
    first = lax.div(t * visits_all, tiles)

    def needs(tile, v):
        start = lax.div(tile * visits_all, tiles)
        return lax.rem(g * visits + v - start + visits_all, visits_all) < DEPTH_MAX

    def gives(group):
        o = lax.rem(group - lax.div(first, visits) + groups, groups)
        return (o * visits - lax.rem(first, visits)) < DEPTH_MAX

    barrier = pltpu.get_barrier_semaphore()

    @pl.when(t > 0)
    def _():
        pl.semaphore_signal(barrier, inc=1, device_id=(t - 1, g), device_id_type=MESH)

    @pl.when(t < tiles - 1)
    def _():
        pl.semaphore_signal(barrier, inc=1, device_id=(t + 1, g), device_id_type=MESH)

    for d in range(1, groups):
        pl.semaphore_signal(
            barrier, inc=1, device_id=(t, lax.rem(g + d, groups)), device_id_type=MESH
        )

    def img_copy(v):
        return pltpu.make_async_copy(
            img_ref.at[v], buf.at[v, pl.ds(0, rows), body], img_sem.at[v]
        )

    def inv_copy(v):
        return pltpu.make_async_copy(
            inv_ref.at[v], inv.at[v, :, pl.ds(0, cols)], inv_sem.at[v]
        )

    def start_local(v, carry):
        @pl.when(needs(t, v))
        def _():
            img_copy(v).start()
            inv_copy(v).start()

        return carry

    lax.fori_loop(0, visits, start_local, 0)

    def clear(v, carry):
        buf[v, :, :LANE] = jnp.zeros((deep, LANE), jnp.bfloat16)
        buf[v, :, LANE + cols :] = jnp.zeros((deep, width - LANE - cols), jnp.bfloat16)
        inv[v, :, cols:] = jnp.zeros((rows, inv.shape[2] - cols), jnp.bfloat16)

        @pl.when(t == 0)
        def _():
            buf[v, rows + EDGE :, LANE : LANE + cols] = jnp.zeros((EDGE, cols), jnp.bfloat16)

        @pl.when(t == tiles - 1)
        def _():
            buf[v, rows : rows + EDGE, LANE : LANE + cols] = jnp.zeros((EDGE, cols), jnp.bfloat16)

        return carry

    lax.fori_loop(0, visits, clear, 0)

    lower = jnp.where(t > 0, 1, 0)
    upper = jnp.where(t < tiles - 1, 1, 0)
    pl.semaphore_wait(barrier, groups - 1 + lower + upper)

    def to_next(v):
        return pltpu.make_async_remote_copy(
            src_ref=img_ref.at[v, pl.ds(rows - EDGE, EDGE)],
            dst_ref=buf.at[v, pl.ds(rows + EDGE, EDGE), body],
            send_sem=halo_send.at[0, v],
            recv_sem=halo_recv.at[0, v],
            device_id=(lax.rem(t + 1, tiles), g),
            device_id_type=MESH,
        )

    def to_last(v):
        return pltpu.make_async_remote_copy(
            src_ref=img_ref.at[v, pl.ds(0, EDGE)],
            dst_ref=buf.at[v, pl.ds(rows, EDGE), body],
            send_sem=halo_send.at[1, v],
            recv_sem=halo_recv.at[1, v],
            device_id=(lax.rem(t + tiles - 1, tiles), g),
            device_id_type=MESH,
        )

    def sends(v, act):
        @pl.when((t < tiles - 1) & needs(t + 1, v))
        def _():
            act(to_next(v))

        @pl.when((t > 0) & needs(t - 1, v))
        def _():
            act(to_last(v))

    def start_halo(v, carry):
        sends(v, lambda c: c.start())
        return carry

    lax.fori_loop(0, visits, start_halo, 0)

    def one_table(k, carry):
        def spread(which, count):
            line = jnp.broadcast_to(base_ref[k, pl.ds(which, 1), :], (count, WIN))
            return pltpu.roll(line, 0, 1, stride=1, stride_axis=0)

        own = spread(0, rows)[:, :LANE]
        above = spread(1, rows)[:, LANE:]
        both = jnp.concatenate([own, above], axis=1).astype(jnp.bfloat16)
        row_tab[k] = both[:, :deep]
        col_tab[k] = spread(2, WIN).astype(jnp.bfloat16)
        return carry

    lax.fori_loop(0, basis, one_table, 0)
    flat[...] = jnp.zeros_like(flat)

    row_ids = t * rows + lax.broadcasted_iota(jnp.int32, (rows, LANE), 0)
    row_coord = (2.0 * row_ids.astype(jnp.float32) + 1.0) / total_rows - 1.0
    row_coord = jnp.concatenate([row_coord] * (WIN // LANE), axis=1)[None]
    lane = lax.broadcasted_iota(jnp.int32, (PAIR, 1, WIN), 2)
    place = lax.broadcasted_iota(jnp.int32, (PAIR, 1, WIN), 0)

    def window(ref, v, at):
        base = pl.multiple_of(lax.div(at, LANE) * LANE, LANE)
        chunk = ref[v, :, pl.ds(base, WIN + LANE)].astype(jnp.float32)
        turn = lax.rem(WIN + LANE - lax.rem(at, LANE), WIN + LANE)
        return pltpu.roll(chunk, turn, 1)[:, :WIN]

    ascend = g >= groups // 2

    def one_pair(s, carry):
        q = jnp.where(ascend, s, pairs - 1 - s)
        acc[...] = jnp.zeros_like(acc)
        col_ids = (q * PAIR + place) * step + lane
        col_coord = (2.0 * col_ids.astype(jnp.float32) + 1.0) / cols - 1.0

        def one_visit(v, inner):
            @pl.when(needs(t, v))
            def _():
                @pl.when(s == 0)
                def _():
                    img_copy(v).wait()
                    inv_copy(v).wait()

                    @pl.when(t > 0)
                    def _():
                        to_next(v).wait_recv()

                    @pl.when(t < tiles - 1)
                    def _():
                        to_last(v).wait_recv()

                who = g * visits + v
                shift = shift_ref[who]
                on = lax.rem(who - first + visits_all, visits_all) < depth_ref[0]
                scale = jnp.where(on, 1.0, 0.0)
                weights = []
                for j in range(PAIR):
                    at = (q * PAIR + j) * step
                    tall = window(buf, v, at + LANE - (WIN - step) // 2)
                    made = jnp.dot(
                        row_tab[...].reshape(basis * rows, deep),
                        tall.astype(jnp.bfloat16),
                        preferred_element_type=jnp.float32,
                    )
                    passed[:, j] = made.astype(jnp.bfloat16).reshape(basis, rows, WIN)
                    weights.append(window(inv, v, at))
                matched = jnp.zeros((PAIR, rows, WIN), jnp.float32)
                for k in range(basis):
                    image = jnp.dot(
                        passed[k].reshape(PAIR * rows, WIN),
                        col_tab[k],
                        preferred_element_type=jnp.float32,
                    ).reshape(PAIR, rows, WIN)
                    c0 = coef_ref[(who * basis + k) * 3]
                    c1 = coef_ref[(who * basis + k) * 3 + 1]
                    c2 = coef_ref[(who * basis + k) * 3 + 2]
                    matched = matched + ((c0 + c1 * col_coord) + c2 * row_coord) * image
                inside = (col_ids >= shift) & (col_ids < shift + cols - DITHER) & (lane < step)
                weight = jnp.stack(weights) * jnp.where(inside, scale, 0.0)
                acc[0] += weight * matched
                acc[1] += weight

            return inner

        lax.fori_loop(0, visits, one_visit, 0)

        @pl.when(gives(g))
        def _():
            for j in range(PAIR):
                at = (q * PAIR + j) * step
                base = pl.multiple_of(lax.div(at, LANE) * LANE, LANE)
                for n in range(2):
                    part = acc[n, j]
                    part = jnp.concatenate([part, jnp.zeros((rows, LANE), jnp.float32)], axis=1)
                    flat[n, :, pl.ds(base, WIN + LANE)] += pltpu.roll(part, lax.rem(at, LANE), 1)

            c = jnp.where(ascend, s - 1, pairs - 1 - s)

            @pl.when((s > 0) & (c != g))
            def _():
                d = lax.rem(c - g + groups, groups)
                for n in range(2):
                    here = flat[n, :, pl.ds(pl.multiple_of(c * strip, LANE), strip)]
                    outgo[d - 1, n] = here.astype(jnp.bfloat16)
                part_copy(d).start()

        return carry

    def part_copy(d):
        return pltpu.make_async_remote_copy(
            src_ref=outgo.at[d - 1],
            dst_ref=income.at[d - 1],
            send_sem=part_send.at[d - 1],
            recv_sem=part_recv.at[d - 1],
            device_id=(t, lax.rem(g + d, groups)),
            device_id_type=MESH,
        )

    lax.fori_loop(0, pairs, one_pair, 0)

    mine = pl.ds(pl.multiple_of(g * strip, LANE), strip)
    for d in range(1, groups):
        @pl.when(gives(lax.rem(g - d + groups, groups)))
        def _():
            part_copy(d).wait_recv()
            for n in range(2):
                flat[n, :, mine] += income[d - 1, n].astype(jnp.float32)

    out_ref[...] = flat[0, :, mine] / (1.0 + flat[1, :, mine])

    @pl.when(gives(g))
    def _():
        for d in range(1, groups):
            part_copy(d).wait_send()

    def end_halo(v, carry):
        sends(v, lambda c: c.wait_send())
        return carry

    lax.fori_loop(0, visits, end_halo, 0)


def local(images, inv_var, row_taps, col_taps, coeffs, dithers, depths):
    visits, rows, cols = images.shape
    basis, taps = row_taps.shape
    tiles = lax.axis_size("sky")
    groups = lax.axis_size("visit")
    step = WIN - taps + 1
    pairs = groups + 1
    strip = cols // groups
    room = cols + WIN
    deep = rows + 2 * EDGE
    bases = base_rows(row_taps, col_taps, rows)
    sizes = (tiles, groups, step)

    def run(*refs):
        kernel(sizes, *refs)

    smem = pl.BlockSpec(memory_space=pltpu.SMEM)
    vmem = pl.BlockSpec(memory_space=pltpu.VMEM)
    hbm = pl.BlockSpec(memory_space=pl.ANY)
    dma = pltpu.SemaphoreType.DMA
    flops = 2 * visits * pairs * PAIR * 2 * basis * rows * WIN * WIN
    return pl.pallas_call(
        run,
        out_shape=jax.ShapeDtypeStruct((rows, strip), jnp.float32),
        in_specs=[smem, smem, smem, vmem, hbm, hbm],
        out_specs=vmem,
        scratch_shapes=[
            pltpu.VMEM((visits, deep, LANE + cols + WIN), jnp.bfloat16),
            pltpu.VMEM((visits, rows, room), jnp.bfloat16),
            pltpu.VMEM((basis, rows, deep), jnp.bfloat16),
            pltpu.VMEM((basis, WIN, WIN), jnp.bfloat16),
            pltpu.VMEM((basis, PAIR, rows, WIN), jnp.bfloat16),
            pltpu.VMEM((2, PAIR, rows, WIN), jnp.float32),
            pltpu.VMEM((2, rows, room), jnp.float32),
            pltpu.VMEM((groups - 1, 2, rows, strip), jnp.bfloat16),
            pltpu.VMEM((groups - 1, 2, rows, strip), jnp.bfloat16),
            dma((visits,)),
            dma((visits,)),
            dma((2, visits)),
            dma((2, visits)),
            dma((groups - 1,)),
            dma((groups - 1,)),
        ],
        compiler_params=pltpu.CompilerParams(
            vmem_limit_bytes=48 * 1024 * 1024, collective_id=0, has_side_effects=True
        ),
        cost_estimate=pl.CostEstimate(
            flops=flops, bytes_accessed=4 * visits * rows * cols, transcendentals=0
        ),
    )(coeffs.reshape(-1), dithers, depths, bases, images, inv_var)


def solution(mesh):
    placed = (P("visit", "sky", None), P("visit", "sky", None), P(), P(), P(), P(), P("sky"))
    return jax.shard_map(
        local, mesh=mesh, in_specs=placed, out_specs=P("sky", "visit"), check_vma=False
    )
```

```python
import jax
import jax.numpy as jnp
from jax import lax
from jax.experimental import pallas as pl
from jax.experimental.pallas import tpu as pltpu
from jax.sharding import PartitionSpec as P

DITHER = 256
DEPTH_MAX = 16
WIN = 256
PAIR = 2
LANE = 128
EDGE = 32
MESH = pl.DeviceIdType.MESH


def kernel(
    sizes,
    coef_ref, shift_ref, depth_ref, row_ref, col_ref, img_ref, inv_ref,
    out_ref,
    buf, inv, base_ref, row_tab, col_tab, pass_a, pass_b, acc, flat, outgo, income,
    img_sem, inv_sem, halo_send, halo_recv, part_send, part_recv,
):
    tiles, groups, step = sizes
    visits, rows, cols = img_ref.shape
    basis, taps = row_ref.shape
    half = taps // 2
    visits_all = visits * groups
    total_rows = rows * tiles
    strip = cols // groups
    width = buf.shape[2]
    deep = rows + 2 * EDGE
    pairs = groups + 1
    body = pl.ds(LANE, cols)

    t = lax.axis_index("sky")
    g = lax.axis_index("visit")
    first = lax.div(t * visits_all, tiles)

    def needs(tile, v):
        start = lax.div(tile * visits_all, tiles)
        return lax.rem(g * visits + v - start + visits_all, visits_all) < DEPTH_MAX

    turn = lax.rem(g - lax.div(first, visits) + groups, groups)
    part = lax.rem(first, visits)
    lo = jnp.where(turn == 0, part, 0)
    hi = jnp.clip(DEPTH_MAX + part - turn * visits, 0, visits)
    twos = lax.div(jnp.maximum(hi - lo, 0) + 1, 2)
    ascend = g >= groups // 2

    def gives(group):
        o = lax.rem(group - lax.div(first, visits) + groups, groups)
        return (o * visits - lax.rem(first, visits)) < DEPTH_MAX

    barrier = pltpu.get_barrier_semaphore()

    @pl.when(t > 0)
    def _():
        pl.semaphore_signal(barrier, inc=1, device_id=(t - 1, g), device_id_type=MESH)

    @pl.when(t < tiles - 1)
    def _():
        pl.semaphore_signal(barrier, inc=1, device_id=(t + 1, g), device_id_type=MESH)

    for d in range(1, groups):
        pl.semaphore_signal(
            barrier, inc=1, device_id=(t, lax.rem(g + d, groups)), device_id_type=MESH
        )

    def img_copy(v):
        return pltpu.make_async_copy(
            img_ref.at[v], buf.at[v, pl.ds(0, rows), body], img_sem.at[v]
        )

    def inv_copy(v):
        return pltpu.make_async_copy(
            inv_ref.at[v], inv.at[v, :, pl.ds(0, cols)], inv_sem.at[v]
        )

    def start_local(v, carry):
        @pl.when(needs(t, v))
        def _():
            img_copy(v).start()
            inv_copy(v).start()

        return carry

    lax.fori_loop(0, visits, start_local, 0)

    def clear(v, carry):
        buf[v, :, :LANE] = jnp.zeros((deep, LANE), jnp.bfloat16)
        buf[v, :, LANE + cols :] = jnp.zeros((deep, width - LANE - cols), jnp.bfloat16)
        inv[v, :, cols:] = jnp.zeros((rows, inv.shape[2] - cols), jnp.bfloat16)

        @pl.when(t == 0)
        def _():
            buf[v, rows + EDGE :, LANE : LANE + cols] = jnp.zeros((EDGE, cols), jnp.bfloat16)

        @pl.when(t == tiles - 1)
        def _():
            buf[v, rows : rows + EDGE, LANE : LANE + cols] = jnp.zeros((EDGE, cols), jnp.bfloat16)

        return carry

    lax.fori_loop(0, visits, clear, 0)

    lower = jnp.where(t > 0, 1, 0)
    upper = jnp.where(t < tiles - 1, 1, 0)
    pl.semaphore_wait(barrier, groups - 1 + lower + upper)

    head = pl.multiple_of(jnp.where(ascend, 0, cols - strip), LANE)
    tail = pl.multiple_of(jnp.where(ascend, strip, 0), LANE)
    spans = ((head, strip), (tail, cols - strip))

    def halo(n, way, v):
        at, size = spans[n]
        if way == 0:
            here, there, tile = rows - EDGE, rows + EDGE, lax.rem(t + 1, tiles)
        else:
            here, there, tile = 0, rows, lax.rem(t + tiles - 1, tiles)
        return pltpu.make_async_remote_copy(
            src_ref=img_ref.at[v, pl.ds(here, EDGE), pl.ds(at, size)],
            dst_ref=buf.at[v, pl.ds(there, EDGE), pl.ds(pl.multiple_of(at + LANE, LANE), size)],
            send_sem=halo_send.at[n, way, v],
            recv_sem=halo_recv.at[n, way, v],
            device_id=(tile, g),
            device_id_type=MESH,
        )

    def sends(n, v, act):
        @pl.when((t < tiles - 1) & needs(t + 1, v))
        def _():
            act(halo(n, 0, v))

        @pl.when((t > 0) & needs(t - 1, v))
        def _():
            act(halo(n, 1, v))

    for n in range(2):
        def start_halo(v, carry):
            sends(n, v, lambda c: c.start())
            return carry

        lax.fori_loop(0, visits, start_halo, 0)

    def arrive(n, v):
        @pl.when(t > 0)
        def _():
            halo(n, 0, v).wait_recv()

        @pl.when(t < tiles - 1)
        def _():
            halo(n, 1, v).wait_recv()

    def ready(v, s):
        @pl.when(s == 0)
        def _():
            img_copy(v).wait()
            inv_copy(v).wait()
            arrive(0, v)

        @pl.when(s == 1)
        def _():
            arrive(1, v)

    spot = lax.broadcasted_iota(jnp.int32, (taps, WIN), 1)
    which = lax.broadcasted_iota(jnp.int32, (taps, WIN), 0)

    def placed(ref, wanted):
        picks = jnp.where(wanted == which, 1.0, 0.0).astype(jnp.bfloat16)
        return jnp.dot(ref[...], picks, preferred_element_type=jnp.float32)

    base_ref[0] = placed(row_ref, jnp.where(spot >= WIN - half, spot - WIN, spot) + half)
    base_ref[1] = placed(row_ref, spot - (LANE + EDGE - half))
    base_ref[2] = placed(col_ref, jnp.where(spot == 0, 0, WIN - spot))

    def one_table(k, carry):
        def spread(n, count):
            line = jnp.broadcast_to(base_ref[n, pl.ds(k, 1), :], (count, WIN))
            return pltpu.roll(line, 0, 1, stride=1, stride_axis=0)

        own = spread(0, rows)[:, :LANE]
        above = spread(1, rows)[:, LANE:]
        both = jnp.concatenate([own, above], axis=1).astype(jnp.bfloat16)
        row_tab[k] = both[:, :deep]
        col_tab[k] = spread(2, WIN).astype(jnp.bfloat16)
        return carry

    lax.fori_loop(0, basis, one_table, 0)
    flat[...] = jnp.zeros_like(flat)

    row_ids = t * rows + lax.broadcasted_iota(jnp.int32, (rows, LANE), 0)
    row_coord = (2.0 * row_ids.astype(jnp.float32) + 1.0) / total_rows - 1.0
    row_coord = jnp.concatenate([row_coord] * (WIN // LANE), axis=1)[None]
    lane = lax.broadcasted_iota(jnp.int32, (PAIR, 1, WIN), 2)
    place = lax.broadcasted_iota(jnp.int32, (PAIR, 1, WIN), 0)

    def window(ref, v, at):
        base = pl.multiple_of(lax.div(at, LANE) * LANE, LANE)
        chunk = ref[v, :, pl.ds(base, WIN + LANE)].astype(jnp.float32)
        turn = lax.rem(WIN + LANE - lax.rem(at, LANE), WIN + LANE)
        return pltpu.roll(chunk, turn, 1)[:, :WIN]

    def place_of(s):
        return jnp.where(ascend, s, pairs - 1 - s)

    def row_windows(v, q):
        return [
            window(buf, v, (q * PAIR + j) * step + LANE - half).astype(jnp.bfloat16)
            for j in range(PAIR)
        ]

    def row_half(dst, tall, j):
        made = jnp.dot(
            row_tab[...].reshape(basis * rows, deep), tall[j], preferred_element_type=jnp.float32
        )
        dst[:, j] = made.astype(jnp.bfloat16).reshape(basis, rows, WIN)

    def step_pair(src, v, on, q, dst, v_next, q_next):
        tall = row_windows(v_next, q_next)
        row_half(dst, tall, 0)
        col_ids = (q * PAIR + place) * step + lane
        col_coord = (2.0 * col_ids.astype(jnp.float32) + 1.0) / cols - 1.0
        who = g * visits + v
        shift = shift_ref[who]
        age = lax.rem(who - first + visits_all, visits_all)
        scale = jnp.where((age < depth_ref[0]) & on, 1.0, 0.0)
        matched = jnp.zeros((PAIR, rows, WIN), jnp.float32)
        for k in range(basis):
            if k == basis // 2:
                row_half(dst, tall, 1)
            image = jnp.dot(
                src[k].reshape(PAIR * rows, WIN), col_tab[k], preferred_element_type=jnp.float32
            ).reshape(PAIR, rows, WIN)
            c0 = coef_ref[k, 0, who]
            c1 = coef_ref[k, 1, who]
            c2 = coef_ref[k, 2, who]
            matched = matched + ((c0 + c1 * col_coord) + c2 * row_coord) * image
        weight = jnp.stack([window(inv, v, (q * PAIR + j) * step) for j in range(PAIR)])
        inside = (col_ids >= shift) & (col_ids < shift + cols - DITHER) & (lane < step)
        weight = weight * jnp.where(inside, scale, 0.0)
        acc[0] += weight * matched
        acc[1] += weight

    @pl.when(twos > 0)
    def _():
        ready(lo, 0)
        tall = row_windows(lo, place_of(0))
        row_half(pass_a, tall, 0)
        row_half(pass_a, tall, 1)

    def one_pair(s, carry):
        q = place_of(s)
        acc[...] = jnp.zeros_like(acc)

        def two_visits(i, inner):
            va = lo + 2 * i
            more = va + 1 < hi
            vb = jnp.where(more, va + 1, va)
            final = i == twos - 1
            vn = jnp.where(final, lo, va + 2)
            sn = jnp.where(final, jnp.minimum(s + 1, pairs - 1), s)

            @pl.when(more)
            def _():
                ready(vb, s)

            @pl.when(jnp.logical_not(final) | (s < pairs - 1))
            def _():
                ready(vn, sn)

            step_pair(pass_a, va, True, q, pass_b, vb, q)
            step_pair(pass_b, vb, more, q, pass_a, vn, place_of(sn))
            return inner

        lax.fori_loop(0, twos, two_visits, 0)

        @pl.when(gives(g))
        def _():
            for j in range(PAIR):
                at = (q * PAIR + j) * step
                base = pl.multiple_of(lax.div(at, LANE) * LANE, LANE)
                for n in range(2):
                    part = acc[n, j]
                    part = jnp.concatenate([part, jnp.zeros((rows, LANE), jnp.float32)], axis=1)
                    flat[n, :, pl.ds(base, WIN + LANE)] += pltpu.roll(part, lax.rem(at, LANE), 1)

            c = jnp.where(ascend, s - 1, pairs - 1 - s)

            @pl.when((s > 0) & (c != g))
            def _():
                d = lax.rem(c - g + groups, groups)
                for n in range(2):
                    here = flat[n, :, pl.ds(pl.multiple_of(c * strip, LANE), strip)]
                    outgo[d - 1, n] = here.astype(jnp.bfloat16)
                part_copy(d).start()

        return carry

    def part_copy(d):
        return pltpu.make_async_remote_copy(
            src_ref=outgo.at[d - 1],
            dst_ref=income.at[d - 1],
            send_sem=part_send.at[d - 1],
            recv_sem=part_recv.at[d - 1],
            device_id=(t, lax.rem(g + d, groups)),
            device_id_type=MESH,
        )

    lax.fori_loop(0, pairs, one_pair, 0)

    mine = pl.ds(pl.multiple_of(g * strip, LANE), strip)
    for d in range(1, groups):
        @pl.when(gives(lax.rem(g - d + groups, groups)))
        def _():
            part_copy(d).wait_recv()
            for n in range(2):
                flat[n, :, mine] += income[d - 1, n].astype(jnp.float32)

    out_ref[...] = flat[0, :, mine] / (1.0 + flat[1, :, mine])

    @pl.when(gives(g))
    def _():
        for d in range(1, groups):
            part_copy(d).wait_send()

    for n in range(2):
        def end_halo(v, carry):
            sends(n, v, lambda c: c.wait_send())
            return carry

        lax.fori_loop(0, visits, end_halo, 0)


def local(images, inv_var, row_taps, col_taps, coeffs, dithers, depths):
    visits, rows, cols = images.shape
    basis, taps = row_taps.shape
    tiles = lax.axis_size("sky")
    groups = lax.axis_size("visit")
    step = WIN - taps + 1
    pairs = groups + 1
    strip = cols // groups
    room = cols + WIN
    deep = rows + 2 * EDGE
    sizes = (tiles, groups, step)

    def run(*refs):
        kernel(sizes, *refs)

    smem = pl.BlockSpec(memory_space=pltpu.SMEM)
    vmem = pl.BlockSpec(memory_space=pltpu.VMEM)
    hbm = pl.BlockSpec(memory_space=pl.ANY)
    dma = pltpu.SemaphoreType.DMA
    flops = 2 * visits * pairs * PAIR * 2 * basis * rows * WIN * WIN
    return pl.pallas_call(
        run,
        out_shape=jax.ShapeDtypeStruct((rows, strip), jnp.float32),
        in_specs=[smem, smem, smem, vmem, vmem, hbm, hbm],
        out_specs=vmem,
        scratch_shapes=[
            pltpu.VMEM((visits, deep, LANE + cols + WIN), jnp.bfloat16),
            pltpu.VMEM((visits, rows, room), jnp.bfloat16),
            pltpu.VMEM((3, basis, WIN), jnp.float32),
            pltpu.VMEM((basis, rows, deep), jnp.bfloat16),
            pltpu.VMEM((basis, WIN, WIN), jnp.bfloat16),
            pltpu.VMEM((basis, PAIR, rows, WIN), jnp.bfloat16),
            pltpu.VMEM((basis, PAIR, rows, WIN), jnp.bfloat16),
            pltpu.VMEM((2, PAIR, rows, WIN), jnp.float32),
            pltpu.VMEM((2, rows, room), jnp.float32),
            pltpu.VMEM((groups - 1, 2, rows, strip), jnp.bfloat16),
            pltpu.VMEM((groups - 1, 2, rows, strip), jnp.bfloat16),
            dma((visits,)),
            dma((visits,)),
            dma((2, 2, visits)),
            dma((2, 2, visits)),
            dma((groups - 1,)),
            dma((groups - 1,)),
        ],
        compiler_params=pltpu.CompilerParams(
            vmem_limit_bytes=60 * 1024 * 1024, collective_id=0, has_side_effects=True
        ),
        cost_estimate=pl.CostEstimate(
            flops=flops, bytes_accessed=4 * visits * rows * cols, transcendentals=0
        ),
    )(jnp.transpose(coeffs, (1, 2, 0)), dithers, depths, row_taps, col_taps, images, inv_var)


def solution(mesh):
    placed = (P("visit", "sky", None), P("visit", "sky", None), P(), P(), P(), P(), P("sky"))
    return jax.shard_map(
        local, mesh=mesh, in_specs=placed, out_specs=P("sky", "visit"), check_vma=False
    )
```

```python
import jax
import jax.numpy as jnp
from jax import lax
from jax.experimental import pallas as pl
from jax.experimental.pallas import tpu as pltpu
from jax.sharding import PartitionSpec as P

DITHER = 256
DEPTH_MAX = 16
WIN = 256
PAIR = 2
LANE = 128
EDGE = 32
MESH = pl.DeviceIdType.MESH


def kernel(
    sizes,
    coef_ref, shift_ref, depth_ref, row_ref, col_ref, img_ref, inv_ref,
    out_ref,
    buf, inv, base_ref, row_tab, col_tab, pass_a, pass_b, acc, flat, outgo, income,
    img_sem, inv_sem, halo_send, halo_recv, part_send, part_recv,
):
    tiles, groups, step = sizes
    visits, rows, cols = img_ref.shape
    basis, taps = row_ref.shape
    half = taps // 2
    visits_all = visits * groups
    total_rows = rows * tiles
    strip = cols // groups
    width = buf.shape[2]
    deep = rows + 2 * EDGE
    pairs = groups + 1
    body = pl.ds(LANE, cols)

    t = lax.axis_index("sky")
    g = lax.axis_index("visit")
    first = lax.div(t * visits_all, tiles)

    def needs(tile, v):
        start = lax.div(tile * visits_all, tiles)
        return lax.rem(g * visits + v - start + visits_all, visits_all) < DEPTH_MAX

    turn = lax.rem(g - lax.div(first, visits) + groups, groups)
    part = lax.rem(first, visits)
    lo = jnp.where(turn == 0, part, 0)
    hi = jnp.clip(DEPTH_MAX + part - turn * visits, 0, visits)
    twos = lax.div(jnp.maximum(hi - lo, 0) + 1, 2)
    ascend = g >= groups // 2

    def gives(group):
        o = lax.rem(group - lax.div(first, visits) + groups, groups)
        return (o * visits - lax.rem(first, visits)) < DEPTH_MAX

    barrier = pltpu.get_barrier_semaphore()

    @pl.when(t > 0)
    def _():
        pl.semaphore_signal(barrier, inc=1, device_id=(t - 1, g), device_id_type=MESH)

    @pl.when(t < tiles - 1)
    def _():
        pl.semaphore_signal(barrier, inc=1, device_id=(t + 1, g), device_id_type=MESH)

    for d in range(1, groups):
        pl.semaphore_signal(
            barrier, inc=1, device_id=(t, lax.rem(g + d, groups)), device_id_type=MESH
        )

    def img_copy(v):
        return pltpu.make_async_copy(
            img_ref.at[v], buf.at[v, pl.ds(0, rows), body], img_sem.at[v]
        )

    def inv_copy(v):
        return pltpu.make_async_copy(
            inv_ref.at[v], inv.at[v, :, pl.ds(0, cols)], inv_sem.at[v]
        )

    def start_local(v, carry):
        @pl.when(needs(t, v))
        def _():
            img_copy(v).start()
            inv_copy(v).start()

        return carry

    lax.fori_loop(0, visits, start_local, 0)

    def clear(v, carry):
        buf[v, :, :LANE] = jnp.zeros((deep, LANE), jnp.bfloat16)
        buf[v, :, LANE + cols :] = jnp.zeros((deep, width - LANE - cols), jnp.bfloat16)
        inv[v, :, cols:] = jnp.zeros((rows, inv.shape[2] - cols), jnp.bfloat16)

        @pl.when(t == 0)
        def _():
            buf[v, rows + EDGE :, LANE : LANE + cols] = jnp.zeros((EDGE, cols), jnp.bfloat16)

        @pl.when(t == tiles - 1)
        def _():
            buf[v, rows : rows + EDGE, LANE : LANE + cols] = jnp.zeros((EDGE, cols), jnp.bfloat16)

        return carry

    lax.fori_loop(0, visits, clear, 0)

    lower = jnp.where(t > 0, 1, 0)
    upper = jnp.where(t < tiles - 1, 1, 0)
    pl.semaphore_wait(barrier, groups - 1 + lower + upper)

    head = pl.multiple_of(jnp.where(ascend, 0, cols - strip), LANE)
    tail = pl.multiple_of(jnp.where(ascend, strip, 0), LANE)
    spans = ((head, strip), (tail, cols - strip))

    def halo(n, way, v):
        at, size = spans[n]
        if way == 0:
            here, there, tile = rows - EDGE, rows + EDGE, lax.rem(t + 1, tiles)
        else:
            here, there, tile = 0, rows, lax.rem(t + tiles - 1, tiles)
        return pltpu.make_async_remote_copy(
            src_ref=img_ref.at[v, pl.ds(here, EDGE), pl.ds(at, size)],
            dst_ref=buf.at[v, pl.ds(there, EDGE), pl.ds(pl.multiple_of(at + LANE, LANE), size)],
            send_sem=halo_send.at[n, way, v],
            recv_sem=halo_recv.at[n, way, v],
            device_id=(tile, g),
            device_id_type=MESH,
        )

    def sends(n, v, act):
        @pl.when((t < tiles - 1) & needs(t + 1, v))
        def _():
            act(halo(n, 0, v))

        @pl.when((t > 0) & needs(t - 1, v))
        def _():
            act(halo(n, 1, v))

    for n in range(2):
        def start_halo(v, carry):
            sends(n, v, lambda c: c.start())
            return carry

        lax.fori_loop(0, visits, start_halo, 0)

    def arrive(n, v):
        @pl.when(t > 0)
        def _():
            halo(n, 0, v).wait_recv()

        @pl.when(t < tiles - 1)
        def _():
            halo(n, 1, v).wait_recv()

    def ready(v, s):
        @pl.when(s == 0)
        def _():
            img_copy(v).wait()
            inv_copy(v).wait()
            arrive(0, v)

        @pl.when(s == 1)
        def _():
            arrive(1, v)

    spot = lax.broadcasted_iota(jnp.int32, (taps, WIN), 1)
    which = lax.broadcasted_iota(jnp.int32, (taps, WIN), 0)

    def placed(ref, wanted):
        picks = jnp.where(wanted == which, 1.0, 0.0).astype(jnp.bfloat16)
        return jnp.dot(ref[...], picks, preferred_element_type=jnp.float32)

    base_ref[0] = placed(row_ref, jnp.where(spot >= WIN - half, spot - WIN, spot) + half)
    base_ref[1] = placed(row_ref, spot - (LANE + EDGE - half))
    base_ref[2] = placed(col_ref, jnp.where(spot == 0, 0, WIN - spot))

    def one_table(k, carry):
        def spread(n, count):
            line = jnp.broadcast_to(base_ref[n, pl.ds(k, 1), :], (count, WIN))
            return pltpu.roll(line, 0, 1, stride=1, stride_axis=0)

        own = spread(0, rows)[:, :LANE]
        above = spread(1, rows)[:, LANE:]
        both = jnp.concatenate([own, above], axis=1).astype(jnp.bfloat16)
        row_tab[pl.ds(pl.multiple_of(k * rows, 32), rows)] = both[:, :deep]
        col_tab[k] = spread(2, WIN).astype(jnp.bfloat16)
        return carry

    lax.fori_loop(0, basis, one_table, 0)
    flat[...] = jnp.zeros_like(flat)

    row_ids = t * rows + lax.broadcasted_iota(jnp.int32, (rows, LANE), 0)
    row_coord = (2.0 * row_ids.astype(jnp.float32) + 1.0) / total_rows - 1.0
    row_coord = jnp.concatenate([row_coord] * (WIN // LANE), axis=1)
    lane = lax.broadcasted_iota(jnp.int32, (1, WIN), 1)

    def window(ref, v, at):
        base = pl.multiple_of(lax.div(at, LANE) * LANE, LANE)
        chunk = ref[v, :, pl.ds(base, WIN + LANE)].astype(jnp.float32)
        turn = lax.rem(WIN + LANE - lax.rem(at, LANE), WIN + LANE)
        return pltpu.roll(chunk, turn, 1)[:, :WIN]

    def place_of(s):
        return jnp.where(ascend, s, pairs - 1 - s)

    def row_windows(v, q):
        return [
            window(buf, v, (q * PAIR + j) * step + LANE - half).astype(jnp.bfloat16)
            for j in range(PAIR)
        ]

    cuts = 3
    chunk = basis * rows // cuts

    def row_chunk(dst, tall, j, n):
        at = pl.ds(n * chunk, chunk)
        made = jnp.dot(row_tab[at, :], tall[j], preferred_element_type=jnp.float32)
        dst[j, at] = made.astype(jnp.bfloat16)

    def row_half(dst, tall, j):
        for n in range(cuts):
            row_chunk(dst, tall, j, n)

    def step_pair(src, v, on, q, dst, v_next, q_next):
        tall = row_windows(v_next, q_next)
        who = g * visits + v
        shift = shift_ref[who]
        age = lax.rem(who - first + visits_all, visits_all)
        scale = jnp.where((age < depth_ref[0]) & on, 1.0, 0.0)
        for j in range(PAIR):
            row_half(dst, tall, j)
            col_ids = (q * PAIR + j) * step + lane
            col_coord = (2.0 * col_ids.astype(jnp.float32) + 1.0) / cols - 1.0
            matched = jnp.zeros((rows, WIN), jnp.float32)
            for k in range(basis):
                image = jnp.dot(
                    src[j, k * rows : (k + 1) * rows], col_tab[k], preferred_element_type=jnp.float32
                )
                c0 = coef_ref[k, 0, who]
                c1 = coef_ref[k, 1, who]
                c2 = coef_ref[k, 2, who]
                matched = matched + ((c0 + c1 * col_coord) + c2 * row_coord) * image
            inside = (col_ids >= shift) & (col_ids < shift + cols - DITHER) & (lane < step)
            weight = window(inv, v, (q * PAIR + j) * step) * jnp.where(inside, scale, 0.0)
            acc[0, j] += weight * matched
            acc[1, j] += weight

    @pl.when(twos > 0)
    def _():
        ready(lo, 0)
        tall = row_windows(lo, place_of(0))
        row_half(pass_a, tall, 0)
        row_half(pass_a, tall, 1)

    def one_pair(s, carry):
        q = place_of(s)
        acc[...] = jnp.zeros_like(acc)

        def two_visits(i, inner):
            va = lo + 2 * i
            more = va + 1 < hi
            vb = jnp.where(more, va + 1, va)
            final = i == twos - 1
            vn = jnp.where(final, lo, va + 2)
            sn = jnp.where(final, jnp.minimum(s + 1, pairs - 1), s)

            @pl.when(more)
            def _():
                ready(vb, s)

            @pl.when(jnp.logical_not(final) | (s < pairs - 1))
            def _():
                ready(vn, sn)

            step_pair(pass_a, va, True, q, pass_b, vb, q)
            step_pair(pass_b, vb, more, q, pass_a, vn, place_of(sn))
            return inner

        lax.fori_loop(0, twos, two_visits, 0)

        @pl.when(gives(g))
        def _():
            for j in range(PAIR):
                at = (q * PAIR + j) * step
                base = pl.multiple_of(lax.div(at, LANE) * LANE, LANE)
                for n in range(2):
                    part = acc[n, j]
                    part = jnp.concatenate([part, jnp.zeros((rows, LANE), jnp.float32)], axis=1)
                    flat[n, :, pl.ds(base, WIN + LANE)] += pltpu.roll(part, lax.rem(at, LANE), 1)

            c = jnp.where(ascend, s - 1, pairs - 1 - s)

            @pl.when((s > 0) & (c != g))
            def _():
                d = lax.rem(c - g + groups, groups)
                for n in range(2):
                    here = flat[n, :, pl.ds(pl.multiple_of(c * strip, LANE), strip)]
                    outgo[d - 1, n] = here.astype(jnp.bfloat16)
                part_copy(d).start()

        return carry

    def part_copy(d):
        return pltpu.make_async_remote_copy(
            src_ref=outgo.at[d - 1],
            dst_ref=income.at[d - 1],
            send_sem=part_send.at[d - 1],
            recv_sem=part_recv.at[d - 1],
            device_id=(t, lax.rem(g + d, groups)),
            device_id_type=MESH,
        )

    lax.fori_loop(0, pairs, one_pair, 0)

    mine = pl.ds(pl.multiple_of(g * strip, LANE), strip)
    for d in range(1, groups):
        @pl.when(gives(lax.rem(g - d + groups, groups)))
        def _():
            part_copy(d).wait_recv()
            for n in range(2):
                flat[n, :, mine] += income[d - 1, n].astype(jnp.float32)

    out_ref[...] = flat[0, :, mine] / (1.0 + flat[1, :, mine])

    @pl.when(gives(g))
    def _():
        for d in range(1, groups):
            part_copy(d).wait_send()

    for n in range(2):
        def end_halo(v, carry):
            sends(n, v, lambda c: c.wait_send())
            return carry

        lax.fori_loop(0, visits, end_halo, 0)


def local(images, inv_var, row_taps, col_taps, coeffs, dithers, depths):
    visits, rows, cols = images.shape
    basis, taps = row_taps.shape
    tiles = lax.axis_size("sky")
    groups = lax.axis_size("visit")
    step = WIN - taps + 1
    pairs = groups + 1
    strip = cols // groups
    room = cols + WIN
    deep = rows + 2 * EDGE
    sizes = (tiles, groups, step)

    def run(*refs):
        kernel(sizes, *refs)

    smem = pl.BlockSpec(memory_space=pltpu.SMEM)
    vmem = pl.BlockSpec(memory_space=pltpu.VMEM)
    hbm = pl.BlockSpec(memory_space=pl.ANY)
    dma = pltpu.SemaphoreType.DMA
    flops = 2 * visits * pairs * PAIR * 2 * basis * rows * WIN * WIN
    return pl.pallas_call(
        run,
        out_shape=jax.ShapeDtypeStruct((rows, strip), jnp.float32),
        in_specs=[smem, smem, smem, vmem, vmem, hbm, hbm],
        out_specs=vmem,
        scratch_shapes=[
            pltpu.VMEM((visits, deep, LANE + cols + WIN), jnp.bfloat16),
            pltpu.VMEM((visits, rows, room), jnp.bfloat16),
            pltpu.VMEM((3, basis, WIN), jnp.float32),
            pltpu.VMEM((basis * rows, deep), jnp.bfloat16),
            pltpu.VMEM((basis, WIN, WIN), jnp.bfloat16),
            pltpu.VMEM((PAIR, basis * rows, WIN), jnp.bfloat16),
            pltpu.VMEM((PAIR, basis * rows, WIN), jnp.bfloat16),
            pltpu.VMEM((2, PAIR, rows, WIN), jnp.float32),
            pltpu.VMEM((2, rows, room), jnp.float32),
            pltpu.VMEM((groups - 1, 2, rows, strip), jnp.bfloat16),
            pltpu.VMEM((groups - 1, 2, rows, strip), jnp.bfloat16),
            dma((visits,)),
            dma((visits,)),
            dma((2, 2, visits)),
            dma((2, 2, visits)),
            dma((groups - 1,)),
            dma((groups - 1,)),
        ],
        compiler_params=pltpu.CompilerParams(
            vmem_limit_bytes=57 * 1024 * 1024, collective_id=0, has_side_effects=True
        ),
        cost_estimate=pl.CostEstimate(
            flops=flops, bytes_accessed=4 * visits * rows * cols, transcendentals=0
        ),
    )(jnp.transpose(coeffs, (1, 2, 0)), dithers, depths, row_taps, col_taps, images, inv_var)


def solution(mesh):
    placed = (P("visit", "sky", None), P("visit", "sky", None), P(), P(), P(), P(), P("sky"))
    return jax.shard_map(
        local, mesh=mesh, in_specs=placed, out_specs=P("sky", "visit"), check_vma=False
    )
```

```python
import jax
import jax.numpy as jnp
from jax import lax
from jax.experimental import pallas as pl
from jax.experimental.pallas import tpu as pltpu
from jax.sharding import PartitionSpec as P

DITHER = 256
DEPTH_MAX = 16
WIN = 256
PAIR = 2
LANE = 128
EDGE = 32
BATCH = 4
MESH = pl.DeviceIdType.MESH


def kernel(
    sizes,
    coef_ref, shift_ref, depth_ref, row_ref, col_ref, img_ref, inv_ref,
    out_ref,
    buf, inv, base_ref, row_tab, col_tab, pass_a, pass_b, acc, flat, outgo, income,
    img_sem, inv_sem, halo_send, halo_recv, part_send, part_recv,
):
    tiles, groups, step = sizes
    visits, rows, cols = img_ref.shape
    basis, taps = row_ref.shape
    half = taps // 2
    visits_all = visits * groups
    total_rows = rows * tiles
    strip = cols // groups
    width = buf.shape[2]
    deep = rows + 2 * EDGE
    pairs = groups + 1
    body = pl.ds(LANE, cols)

    t = lax.axis_index("sky")
    g = lax.axis_index("visit")
    first = lax.div(t * visits_all, tiles)

    def needs(tile, v):
        start = lax.div(tile * visits_all, tiles)
        return lax.rem(g * visits + v - start + visits_all, visits_all) < DEPTH_MAX

    turn = lax.rem(g - lax.div(first, visits) + groups, groups)
    part = lax.rem(first, visits)
    lo = jnp.where(turn == 0, part, 0)
    hi = jnp.clip(DEPTH_MAX + part - turn * visits, 0, visits)
    twos = lax.div(jnp.maximum(hi - lo, 0) + 1, 2)
    ascend = g >= groups // 2

    def gives(group):
        o = lax.rem(group - lax.div(first, visits) + groups, groups)
        return (o * visits - lax.rem(first, visits)) < DEPTH_MAX

    barrier = pltpu.get_barrier_semaphore()

    @pl.when(t > 0)
    def _():
        pl.semaphore_signal(barrier, inc=1, device_id=(t - 1, g), device_id_type=MESH)

    @pl.when(t < tiles - 1)
    def _():
        pl.semaphore_signal(barrier, inc=1, device_id=(t + 1, g), device_id_type=MESH)

    for d in range(1, groups):
        pl.semaphore_signal(
            barrier, inc=1, device_id=(t, lax.rem(g + d, groups)), device_id_type=MESH
        )

    def img_copy(v):
        return pltpu.make_async_copy(
            img_ref.at[v], buf.at[v, pl.ds(0, rows), body], img_sem.at[v]
        )

    def inv_copy(v):
        return pltpu.make_async_copy(
            inv_ref.at[v], inv.at[v, :, pl.ds(0, cols)], inv_sem.at[v]
        )

    def start_local(v, carry):
        @pl.when(needs(t, v))
        def _():
            img_copy(v).start()
            inv_copy(v).start()

        return carry

    lax.fori_loop(0, visits, start_local, 0)

    def clear(v, carry):
        buf[v, :, :LANE] = jnp.zeros((deep, LANE), jnp.bfloat16)
        buf[v, :, LANE + cols :] = jnp.zeros((deep, width - LANE - cols), jnp.bfloat16)
        inv[v, :, cols:] = jnp.zeros((rows, inv.shape[2] - cols), jnp.bfloat16)

        @pl.when(t == 0)
        def _():
            buf[v, rows + EDGE :, LANE : LANE + cols] = jnp.zeros((EDGE, cols), jnp.bfloat16)

        @pl.when(t == tiles - 1)
        def _():
            buf[v, rows : rows + EDGE, LANE : LANE + cols] = jnp.zeros((EDGE, cols), jnp.bfloat16)

        return carry

    lax.fori_loop(0, visits, clear, 0)

    lower = jnp.where(t > 0, 1, 0)
    upper = jnp.where(t < tiles - 1, 1, 0)
    pl.semaphore_wait(barrier, groups - 1 + lower + upper)

    def halo(n, way, b):
        at = pl.multiple_of(jnp.where(ascend, n, groups - 1 - n) * strip, LANE)
        if way == 0:
            here, there, tile = rows - EDGE, rows + EDGE, lax.rem(t + 1, tiles)
        else:
            here, there, tile = 0, rows, lax.rem(t + tiles - 1, tiles)
        some = pl.ds(b * BATCH, BATCH)
        to = pl.ds(pl.multiple_of(at + LANE, LANE), strip)
        return pltpu.make_async_remote_copy(
            src_ref=img_ref.at[some, pl.ds(here, EDGE), pl.ds(at, strip)],
            dst_ref=buf.at[some, pl.ds(there, EDGE), to],
            send_sem=halo_send.at[n, way, b],
            recv_sem=halo_recv.at[n, way, b],
            device_id=(tile, g),
            device_id_type=MESH,
        )

    def needs_any(tile, b):
        found = needs(tile, b * BATCH)
        for r in range(1, BATCH):
            found = found | needs(tile, b * BATCH + r)
        return found

    def sends(n, b, act):
        @pl.when((t < tiles - 1) & needs_any(t + 1, b))
        def _():
            act(halo(n, 0, b))

        @pl.when((t > 0) & needs_any(t - 1, b))
        def _():
            act(halo(n, 1, b))

    def start_halo(n):
        def one_batch(b, carry):
            sends(n, b, lambda c: c.start())
            return carry

        lax.fori_loop(0, visits // BATCH, one_batch, 0)

    start_halo(0)
    start_halo(1)

    def ready(v, s):
        @pl.when(s == 0)
        def _():
            img_copy(v).wait()
            inv_copy(v).wait()

        @pl.when((s < groups) & ((v == lo) | (lax.rem(v, BATCH) == 0)))
        def _():
            b = lax.div(v, BATCH)

            @pl.when(t > 0)
            def _():
                halo(s, 0, b).wait_recv()

            @pl.when(t < tiles - 1)
            def _():
                halo(s, 1, b).wait_recv()

    spot = lax.broadcasted_iota(jnp.int32, (taps, WIN), 1)
    which = lax.broadcasted_iota(jnp.int32, (taps, WIN), 0)

    def placed(ref, wanted):
        picks = jnp.where(wanted == which, 1.0, 0.0).astype(jnp.bfloat16)
        return jnp.dot(ref[...], picks, preferred_element_type=jnp.float32)

    base_ref[0] = placed(row_ref, jnp.where(spot >= WIN - half, spot - WIN, spot) + half)
    base_ref[1] = placed(row_ref, spot - (LANE + EDGE - half))
    base_ref[2] = placed(col_ref, jnp.where(spot == 0, 0, WIN - spot))

    def one_table(k, carry):
        def spread(n, count):
            line = jnp.broadcast_to(base_ref[n, pl.ds(k, 1), :], (count, WIN))
            return pltpu.roll(line, 0, 1, stride=1, stride_axis=0)

        own = spread(0, rows)[:, :LANE]
        above = spread(1, rows)[:, LANE:]
        both = jnp.concatenate([own, above], axis=1).astype(jnp.bfloat16)
        row_tab[k] = both[:, :deep]
        col_tab[k] = spread(2, WIN).astype(jnp.bfloat16)
        return carry

    lax.fori_loop(0, basis, one_table, 0)
    flat[...] = jnp.zeros_like(flat)

    row_ids = t * rows + lax.broadcasted_iota(jnp.int32, (rows, LANE), 0)
    row_coord = (2.0 * row_ids.astype(jnp.float32) + 1.0) / total_rows - 1.0
    row_coord = jnp.concatenate([row_coord] * (WIN // LANE), axis=1)[None]
    lane = lax.broadcasted_iota(jnp.int32, (PAIR, 1, WIN), 2)
    place = lax.broadcasted_iota(jnp.int32, (PAIR, 1, WIN), 0)

    def window(ref, v, at):
        base = pl.multiple_of(lax.div(at, LANE) * LANE, LANE)
        chunk = ref[v, :, pl.ds(base, WIN + LANE)].astype(jnp.float32)
        turn = lax.rem(WIN + LANE - lax.rem(at, LANE), WIN + LANE)
        return pltpu.roll(chunk, turn, 1)[:, :WIN]

    def place_of(s):
        return jnp.where(ascend, s, pairs - 1 - s)

    def row_windows(v, q):
        return [
            window(buf, v, (q * PAIR + j) * step + LANE - half).astype(jnp.bfloat16)
            for j in range(PAIR)
        ]

    def row_half(dst, tall, j):
        made = jnp.dot(
            row_tab[...].reshape(basis * rows, deep), tall[j], preferred_element_type=jnp.float32
        )
        dst[:, j] = made.astype(jnp.bfloat16).reshape(basis, rows, WIN)

    def step_pair(src, v, on, q, dst, v_next, q_next):
        tall = row_windows(v_next, q_next)
        row_half(dst, tall, 0)
        col_ids = (q * PAIR + place) * step + lane
        col_coord = (2.0 * col_ids.astype(jnp.float32) + 1.0) / cols - 1.0
        who = g * visits + v
        shift = shift_ref[who]
        age = lax.rem(who - first + visits_all, visits_all)
        scale = jnp.where((age < depth_ref[0]) & on, 1.0, 0.0)
        matched = jnp.zeros((PAIR, rows, WIN), jnp.float32)
        for k in range(basis):
            if k == basis // 2:
                row_half(dst, tall, 1)
            image = jnp.dot(
                src[k].reshape(PAIR * rows, WIN), col_tab[k], preferred_element_type=jnp.float32
            ).reshape(PAIR, rows, WIN)
            c0 = coef_ref[k, 0, who]
            c1 = coef_ref[k, 1, who]
            c2 = coef_ref[k, 2, who]
            matched = matched + ((c0 + c1 * col_coord) + c2 * row_coord) * image
        weight = jnp.stack([window(inv, v, (q * PAIR + j) * step) for j in range(PAIR)])
        inside = (col_ids >= shift) & (col_ids < shift + cols - DITHER) & (lane < step)
        weight = weight * jnp.where(inside, scale, 0.0)
        acc[0] += weight * matched
        acc[1] += weight

    @pl.when(twos > 0)
    def _():
        ready(lo, 0)
        tall = row_windows(lo, place_of(0))
        row_half(pass_a, tall, 0)
        row_half(pass_a, tall, 1)

    def one_pair(s, carry):
        q = place_of(s)
        acc[...] = jnp.zeros_like(acc)

        @pl.when(s + 2 < groups)
        def _():
            start_halo(s + 2)

        def two_visits(i, inner):
            va = lo + 2 * i
            more = va + 1 < hi
            vb = jnp.where(more, va + 1, va)
            final = i == twos - 1
            vn = jnp.where(final, lo, va + 2)
            sn = jnp.where(final, jnp.minimum(s + 1, pairs - 1), s)

            @pl.when(more)
            def _():
                ready(vb, s)

            @pl.when(jnp.logical_not(final) | (s < pairs - 1))
            def _():
                ready(vn, sn)

            step_pair(pass_a, va, True, q, pass_b, vb, q)
            step_pair(pass_b, vb, more, q, pass_a, vn, place_of(sn))
            return inner

        lax.fori_loop(0, twos, two_visits, 0)

        @pl.when(gives(g))
        def _():
            for j in range(PAIR):
                at = (q * PAIR + j) * step
                base = pl.multiple_of(lax.div(at, LANE) * LANE, LANE)
                for n in range(2):
                    part = acc[n, j]
                    part = jnp.concatenate([part, jnp.zeros((rows, LANE), jnp.float32)], axis=1)
                    flat[n, :, pl.ds(base, WIN + LANE)] += pltpu.roll(part, lax.rem(at, LANE), 1)

            c = jnp.where(ascend, s - 1, pairs - 1 - s)

            @pl.when((s > 0) & (c != g))
            def _():
                d = lax.rem(c - g + groups, groups)
                for n in range(2):
                    here = flat[n, :, pl.ds(pl.multiple_of(c * strip, LANE), strip)]
                    outgo[d - 1, n] = here.astype(jnp.bfloat16)
                part_copy(d).start()

        return carry

    def part_copy(d):
        return pltpu.make_async_remote_copy(
            src_ref=outgo.at[d - 1],
            dst_ref=income.at[d - 1],
            send_sem=part_send.at[d - 1],
            recv_sem=part_recv.at[d - 1],
            device_id=(t, lax.rem(g + d, groups)),
            device_id_type=MESH,
        )

    lax.fori_loop(0, pairs, one_pair, 0)

    mine = pl.ds(pl.multiple_of(g * strip, LANE), strip)
    for d in range(1, groups):
        @pl.when(gives(lax.rem(g - d + groups, groups)))
        def _():
            part_copy(d).wait_recv()
            for n in range(2):
                flat[n, :, mine] += income[d - 1, n].astype(jnp.float32)

    out_ref[...] = flat[0, :, mine] / (1.0 + flat[1, :, mine])

    @pl.when(gives(g))
    def _():
        for d in range(1, groups):
            part_copy(d).wait_send()

    def end_halo(n, carry):
        def one_batch(b, inner):
            sends(n, b, lambda c: c.wait_send())
            return inner

        lax.fori_loop(0, visits // BATCH, one_batch, 0)
        return carry

    lax.fori_loop(0, groups, end_halo, 0)


def local(images, inv_var, row_taps, col_taps, coeffs, dithers, depths):
    visits, rows, cols = images.shape
    basis, taps = row_taps.shape
    tiles = lax.axis_size("sky")
    groups = lax.axis_size("visit")
    step = WIN - taps + 1
    pairs = groups + 1
    strip = cols // groups
    room = cols + WIN
    deep = rows + 2 * EDGE
    sizes = (tiles, groups, step)

    def run(*refs):
        kernel(sizes, *refs)

    smem = pl.BlockSpec(memory_space=pltpu.SMEM)
    vmem = pl.BlockSpec(memory_space=pltpu.VMEM)
    hbm = pl.BlockSpec(memory_space=pl.ANY)
    dma = pltpu.SemaphoreType.DMA
    flops = 2 * visits * pairs * PAIR * 2 * basis * rows * WIN * WIN
    return pl.pallas_call(
        run,
        out_shape=jax.ShapeDtypeStruct((rows, strip), jnp.float32),
        in_specs=[smem, smem, smem, vmem, vmem, hbm, hbm],
        out_specs=vmem,
        scratch_shapes=[
            pltpu.VMEM((visits, deep, LANE + cols + WIN), jnp.bfloat16),
            pltpu.VMEM((visits, rows, room), jnp.bfloat16),
            pltpu.VMEM((3, basis, WIN), jnp.float32),
            pltpu.VMEM((basis, rows, deep), jnp.bfloat16),
            pltpu.VMEM((basis, WIN, WIN), jnp.bfloat16),
            pltpu.VMEM((basis, PAIR, rows, WIN), jnp.bfloat16),
            pltpu.VMEM((basis, PAIR, rows, WIN), jnp.bfloat16),
            pltpu.VMEM((2, PAIR, rows, WIN), jnp.float32),
            pltpu.VMEM((2, rows, room), jnp.float32),
            pltpu.VMEM((groups - 1, 2, rows, strip), jnp.bfloat16),
            pltpu.VMEM((groups - 1, 2, rows, strip), jnp.bfloat16),
            dma((visits,)),
            dma((visits,)),
            dma((groups, 2, visits // BATCH)),
            dma((groups, 2, visits // BATCH)),
            dma((groups - 1,)),
            dma((groups - 1,)),
        ],
        compiler_params=pltpu.CompilerParams(
            vmem_limit_bytes=55 * 1024 * 1024, collective_id=0, has_side_effects=True
        ),
        cost_estimate=pl.CostEstimate(
            flops=flops, bytes_accessed=4 * visits * rows * cols, transcendentals=0
        ),
    )(jnp.transpose(coeffs, (1, 2, 0)), dithers, depths, row_taps, col_taps, images, inv_var)


def solution(mesh):
    placed = (P("visit", "sky", None), P("visit", "sky", None), P(), P(), P(), P(), P("sky"))
    return jax.shard_map(
        local, mesh=mesh, in_specs=placed, out_specs=P("sky", "visit"), check_vma=False
    )
```

```python
import jax
import jax.numpy as jnp
from jax import lax
from jax.experimental import pallas as pl
from jax.experimental.pallas import tpu as pltpu
from jax.sharding import PartitionSpec as P

DITHER = 256
DEPTH_MAX = 16
WIN = 256
PAIR = 2
LANE = 128
EDGE = 32
BATCH = 4
MESH = pl.DeviceIdType.MESH


def kernel(
    sizes,
    coef_ref, shift_ref, depth_ref, row_ref, col_ref, img_ref, inv_ref,
    out_ref,
    buf, inv, base_ref, row_tab, col_tab, pass_a, pass_b, acc, flat, outgo, income,
    img_sem, inv_sem, halo_send, halo_recv, part_send, part_recv,
):
    tiles, groups, step = sizes
    visits, rows, cols = img_ref.shape
    basis, taps = row_ref.shape
    half = taps // 2
    visits_all = visits * groups
    total_rows = rows * tiles
    strip = cols // groups
    width = buf.shape[2]
    deep = rows + 2 * EDGE
    pairs = groups + 1
    body = pl.ds(LANE, cols)

    t = lax.axis_index("sky")
    g = lax.axis_index("visit")
    first = lax.div(t * visits_all, tiles)

    def needs(tile, v):
        start = lax.div(tile * visits_all, tiles)
        return lax.rem(g * visits + v - start + visits_all, visits_all) < DEPTH_MAX

    turn = lax.rem(g - lax.div(first, visits) + groups, groups)
    part = lax.rem(first, visits)
    lo = jnp.where(turn == 0, part, 0)
    hi = jnp.clip(DEPTH_MAX + part - turn * visits, 0, visits)
    twos = lax.div(jnp.maximum(hi - lo, 0) + 1, 2)
    ascend = g >= groups // 2

    def gives(group):
        o = lax.rem(group - lax.div(first, visits) + groups, groups)
        return (o * visits - lax.rem(first, visits)) < DEPTH_MAX

    barrier = pltpu.get_barrier_semaphore()

    @pl.when(t > 0)
    def _():
        pl.semaphore_signal(barrier, inc=1, device_id=(t - 1, g), device_id_type=MESH)

    @pl.when(t < tiles - 1)
    def _():
        pl.semaphore_signal(barrier, inc=1, device_id=(t + 1, g), device_id_type=MESH)

    for d in range(1, groups):
        pl.semaphore_signal(
            barrier, inc=1, device_id=(t, lax.rem(g + d, groups)), device_id_type=MESH
        )

    def img_copy(v):
        return pltpu.make_async_copy(
            img_ref.at[v], buf.at[v, pl.ds(0, rows), body], img_sem.at[v]
        )

    def inv_copy(v):
        return pltpu.make_async_copy(
            inv_ref.at[v], inv.at[v, :, pl.ds(0, cols)], inv_sem.at[v]
        )

    def start_local(v, carry):
        @pl.when(needs(t, v))
        def _():
            img_copy(v).start()
            inv_copy(v).start()

        return carry

    lax.fori_loop(0, visits, start_local, 0)

    def clear(v, carry):
        buf[v, :, :LANE] = jnp.zeros((deep, LANE), jnp.bfloat16)
        buf[v, :, LANE + cols :] = jnp.zeros((deep, width - LANE - cols), jnp.bfloat16)
        inv[v, :, cols:] = jnp.zeros((rows, inv.shape[2] - cols), jnp.bfloat16)

        @pl.when(t == 0)
        def _():
            buf[v, rows + EDGE :, LANE : LANE + cols] = jnp.zeros((EDGE, cols), jnp.bfloat16)

        @pl.when(t == tiles - 1)
        def _():
            buf[v, rows : rows + EDGE, LANE : LANE + cols] = jnp.zeros((EDGE, cols), jnp.bfloat16)

        return carry

    lax.fori_loop(0, visits, clear, 0)

    lower = jnp.where(t > 0, 1, 0)
    upper = jnp.where(t < tiles - 1, 1, 0)
    pl.semaphore_wait(barrier, groups - 1 + lower + upper)

    def halo(n, way, b):
        at = pl.multiple_of(jnp.where(ascend, n, groups - 1 - n) * strip, LANE)
        if way == 0:
            here, there, tile = rows - EDGE, rows + EDGE, lax.rem(t + 1, tiles)
        else:
            here, there, tile = 0, rows, lax.rem(t + tiles - 1, tiles)
        some = pl.ds(b * BATCH, BATCH)
        to = pl.ds(pl.multiple_of(at + LANE, LANE), strip)
        return pltpu.make_async_remote_copy(
            src_ref=img_ref.at[some, pl.ds(here, EDGE), pl.ds(at, strip)],
            dst_ref=buf.at[some, pl.ds(there, EDGE), to],
            send_sem=halo_send.at[n, way, b],
            recv_sem=halo_recv.at[n, way, b],
            device_id=(tile, g),
            device_id_type=MESH,
        )

    def needs_any(tile, b):
        found = needs(tile, b * BATCH)
        for r in range(1, BATCH):
            found = found | needs(tile, b * BATCH + r)
        return found

    def sends(n, b, act):
        @pl.when((t < tiles - 1) & needs_any(t + 1, b))
        def _():
            act(halo(n, 0, b))

        @pl.when((t > 0) & needs_any(t - 1, b))
        def _():
            act(halo(n, 1, b))

    def start_halo(n):
        def one_batch(b, carry):
            sends(n, b, lambda c: c.start())
            return carry

        lax.fori_loop(0, visits // BATCH, one_batch, 0)

    start_halo(0)
    start_halo(1)

    def ready(v, s):
        @pl.when(s == 0)
        def _():
            img_copy(v).wait()
            inv_copy(v).wait()

        @pl.when((s < groups) & ((v == lo) | (lax.rem(v, BATCH) == 0)))
        def _():
            b = lax.div(v, BATCH)

            @pl.when(t > 0)
            def _():
                halo(s, 0, b).wait_recv()

            @pl.when(t < tiles - 1)
            def _():
                halo(s, 1, b).wait_recv()

    spot = lax.broadcasted_iota(jnp.int32, (taps, WIN), 1)
    which = lax.broadcasted_iota(jnp.int32, (taps, WIN), 0)

    def placed(ref, wanted):
        picks = jnp.where(wanted == which, 1.0, 0.0).astype(jnp.bfloat16)
        return jnp.dot(ref[...], picks, preferred_element_type=jnp.float32)

    base_ref[0] = placed(row_ref, jnp.where(spot >= WIN - half, spot - WIN, spot) + half)
    base_ref[1] = placed(row_ref, spot - (LANE + EDGE - half))
    base_ref[2] = placed(col_ref, jnp.where(spot == 0, 0, WIN - spot))

    for k in range(basis):
        def spread(n, count):
            line = jnp.broadcast_to(base_ref[n, k : k + 1, :], (count, WIN))
            return pltpu.roll(line, 0, 1, stride=1, stride_axis=0)

        own = spread(0, rows)[:, :LANE]
        above = spread(1, rows)[:, LANE:]
        both = jnp.concatenate([own, above], axis=1).astype(jnp.bfloat16)
        row_tab[k] = both[:, :deep]
        col_tab[k] = spread(2, WIN).astype(jnp.bfloat16)

    flat[...] = jnp.zeros_like(flat)

    row_ids = t * rows + lax.broadcasted_iota(jnp.int32, (rows, LANE), 0)
    row_coord = (2.0 * row_ids.astype(jnp.float32) + 1.0) / total_rows - 1.0
    row_coord = jnp.concatenate([row_coord] * (WIN // LANE), axis=1)[None]
    lane = lax.broadcasted_iota(jnp.int32, (PAIR, 1, WIN), 2)
    place = lax.broadcasted_iota(jnp.int32, (PAIR, 1, WIN), 0)

    def window(ref, v, at):
        base = pl.multiple_of(lax.div(at, LANE) * LANE, LANE)
        chunk = ref[v, :, pl.ds(base, WIN + LANE)].astype(jnp.float32)
        turn = lax.rem(WIN + LANE - lax.rem(at, LANE), WIN + LANE)
        return pltpu.roll(chunk, turn, 1)[:, :WIN]

    def place_of(s):
        return jnp.where(ascend, s, pairs - 1 - s)

    def row_windows(v, q):
        return jnp.concatenate(
            [
                window(buf, v, (q * PAIR + j) * step + LANE - half).astype(jnp.bfloat16)
                for j in range(PAIR)
            ],
            axis=1,
        )

    def row_part(dst, tall, k0, k1):
        made = jnp.dot(
            row_tab[k0:k1].reshape((k1 - k0) * rows, deep), tall, preferred_element_type=jnp.float32
        ).astype(jnp.bfloat16)
        for j in range(PAIR):
            dst[k0:k1, j] = made[:, j * WIN : (j + 1) * WIN].reshape(k1 - k0, rows, WIN)

    def step_pair(src, v, on, q, dst, v_next, q_next):
        tall = row_windows(v_next, q_next)
        cut = basis // 2
        row_part(dst, tall, 0, cut)
        col_ids = (q * PAIR + place) * step + lane
        col_coord = (2.0 * col_ids.astype(jnp.float32) + 1.0) / cols - 1.0
        who = g * visits + v
        shift = shift_ref[who]
        age = lax.rem(who - first + visits_all, visits_all)
        scale = jnp.where((age < depth_ref[0]) & on, 1.0, 0.0)
        matched = jnp.zeros((PAIR, rows, WIN), jnp.float32)
        def basis_image(k):
            return jnp.dot(
                src[k].reshape(PAIR * rows, WIN), col_tab[k], preferred_element_type=jnp.float32
            ).reshape(PAIR, rows, WIN)

        def spatial(k):
            c0 = coef_ref[k, 0, who]
            c1 = coef_ref[k, 1, who]
            c2 = coef_ref[k, 2, who]
            return (c0 + c1 * col_coord) + c2 * row_coord

        for k in range(0, basis, 2):
            if k == cut - cut % 2:
                row_part(dst, tall, cut, basis)
            pair = [kk for kk in (k, k + 1) if kk < basis]
            both = [basis_image(kk) for kk in pair]
            for kk, image in zip(pair, both):
                matched = matched + spatial(kk) * image
        weight = jnp.stack([window(inv, v, (q * PAIR + j) * step) for j in range(PAIR)])
        inside = (col_ids >= shift) & (col_ids < shift + cols - DITHER) & (lane < step)
        weight = weight * jnp.where(inside, scale, 0.0)
        acc[0] += weight * matched
        acc[1] += weight

    @pl.when(twos > 0)
    def _():
        ready(lo, 0)
        tall = row_windows(lo, place_of(0))
        row_part(pass_a, tall, 0, basis)

    def one_pair(s, carry):
        q = place_of(s)
        acc[...] = jnp.zeros_like(acc)

        @pl.when(s + 2 < groups)
        def _():
            start_halo(s + 2)

        def two_visits(i, inner):
            va = lo + 2 * i
            more = va + 1 < hi
            vb = jnp.where(more, va + 1, va)
            final = i == twos - 1
            vn = jnp.where(final, lo, va + 2)
            sn = jnp.where(final, jnp.minimum(s + 1, pairs - 1), s)

            @pl.when(more)
            def _():
                ready(vb, s)

            @pl.when(jnp.logical_not(final) | (s < pairs - 1))
            def _():
                ready(vn, sn)

            step_pair(pass_a, va, True, q, pass_b, vb, q)
            step_pair(pass_b, vb, more, q, pass_a, vn, place_of(sn))
            return inner

        lax.fori_loop(0, twos, two_visits, 0)

        @pl.when(gives(g))
        def _():
            for j in range(PAIR):
                at = (q * PAIR + j) * step
                base = pl.multiple_of(lax.div(at, LANE) * LANE, LANE)
                for n in range(2):
                    part = acc[n, j]
                    part = jnp.concatenate([part, jnp.zeros((rows, LANE), jnp.float32)], axis=1)
                    flat[n, :, pl.ds(base, WIN + LANE)] += pltpu.roll(part, lax.rem(at, LANE), 1)

            c = jnp.where(ascend, s - 1, pairs - 1 - s)

            @pl.when((s > 0) & (c != g))
            def _():
                d = lax.rem(c - g + groups, groups)
                for n in range(2):
                    here = flat[n, :, pl.ds(pl.multiple_of(c * strip, LANE), strip)]
                    outgo[d - 1, n] = here.astype(jnp.bfloat16)
                part_copy(d).start()

        return carry

    def part_copy(d):
        return pltpu.make_async_remote_copy(
            src_ref=outgo.at[d - 1],
            dst_ref=income.at[d - 1],
            send_sem=part_send.at[d - 1],
            recv_sem=part_recv.at[d - 1],
            device_id=(t, lax.rem(g + d, groups)),
            device_id_type=MESH,
        )

    lax.fori_loop(0, pairs, one_pair, 0)

    mine = pl.ds(pl.multiple_of(g * strip, LANE), strip)
    for d in range(1, groups):
        @pl.when(gives(lax.rem(g - d + groups, groups)))
        def _():
            part_copy(d).wait_recv()
            for n in range(2):
                flat[n, :, mine] += income[d - 1, n].astype(jnp.float32)

    out_ref[...] = flat[0, :, mine] / (1.0 + flat[1, :, mine])

    @pl.when(gives(g))
    def _():
        for d in range(1, groups):
            part_copy(d).wait_send()

    def end_halo(n, carry):
        def one_batch(b, inner):
            sends(n, b, lambda c: c.wait_send())
            return inner

        lax.fori_loop(0, visits // BATCH, one_batch, 0)
        return carry

    lax.fori_loop(0, groups, end_halo, 0)


def local(images, inv_var, row_taps, col_taps, coeffs, dithers, depths):
    visits, rows, cols = images.shape
    basis, taps = row_taps.shape
    tiles = lax.axis_size("sky")
    groups = lax.axis_size("visit")
    step = WIN - taps + 1
    pairs = groups + 1
    strip = cols // groups
    room = cols + WIN
    deep = rows + 2 * EDGE
    sizes = (tiles, groups, step)

    def run(*refs):
        kernel(sizes, *refs)

    smem = pl.BlockSpec(memory_space=pltpu.SMEM)
    vmem = pl.BlockSpec(memory_space=pltpu.VMEM)
    hbm = pl.BlockSpec(memory_space=pl.ANY)
    dma = pltpu.SemaphoreType.DMA
    flops = 2 * visits * pairs * PAIR * 2 * basis * rows * WIN * WIN
    return pl.pallas_call(
        run,
        out_shape=jax.ShapeDtypeStruct((rows, strip), jnp.float32),
        in_specs=[smem, smem, smem, vmem, vmem, hbm, hbm],
        out_specs=vmem,
        scratch_shapes=[
            pltpu.VMEM((visits, deep, LANE + cols + WIN), jnp.bfloat16),
            pltpu.VMEM((visits, rows, room), jnp.bfloat16),
            pltpu.VMEM((3, basis, WIN), jnp.float32),
            pltpu.VMEM((basis, rows, deep), jnp.bfloat16),
            pltpu.VMEM((basis, WIN, WIN), jnp.bfloat16),
            pltpu.VMEM((basis, PAIR, rows, WIN), jnp.bfloat16),
            pltpu.VMEM((basis, PAIR, rows, WIN), jnp.bfloat16),
            pltpu.VMEM((2, PAIR, rows, WIN), jnp.float32),
            pltpu.VMEM((2, rows, room), jnp.float32),
            pltpu.VMEM((groups - 1, 2, rows, strip), jnp.bfloat16),
            pltpu.VMEM((groups - 1, 2, rows, strip), jnp.bfloat16),
            dma((visits,)),
            dma((visits,)),
            dma((groups, 2, visits // BATCH)),
            dma((groups, 2, visits // BATCH)),
            dma((groups - 1,)),
            dma((groups - 1,)),
        ],
        compiler_params=pltpu.CompilerParams(
            vmem_limit_bytes=55 * 1024 * 1024, collective_id=0, has_side_effects=True
        ),
        cost_estimate=pl.CostEstimate(
            flops=flops, bytes_accessed=4 * visits * rows * cols, transcendentals=0
        ),
    )(jnp.transpose(coeffs, (1, 2, 0)), dithers, depths, row_taps, col_taps, images, inv_var)


def solution(mesh):
    placed = (P("visit", "sky", None), P("visit", "sky", None), P(), P(), P(), P(), P("sky"))
    return jax.shard_map(
        local, mesh=mesh, in_specs=placed, out_specs=P("sky", "visit"), check_vma=False
    )
```

```python
import jax
import jax.numpy as jnp
from jax import lax
from jax.experimental import pallas as pl
from jax.experimental.pallas import tpu as pltpu
from jax.sharding import PartitionSpec as P

DITHER = 256
DEPTH_MAX = 16
WIN = 256
PAIR = 2
LANE = 128
EDGE = 32
BATCH = 4
MESH = pl.DeviceIdType.MESH


def kernel(
    sizes,
    coef_ref, shift_ref, depth_ref, row_ref, col_ref, img_ref, inv_ref,
    out_ref,
    buf, inv, base_ref, row_tab, col_tab, pass_a, pass_b, acc, flat, total, outgo, income,
    img_sem, inv_sem, halo_send, halo_recv, part_send, part_recv,
):
    tiles, groups, step = sizes
    visits, rows, cols = img_ref.shape
    basis, taps = row_ref.shape
    half = taps // 2
    visits_all = visits * groups
    total_rows = rows * tiles
    strip = cols // groups
    width = buf.shape[2]
    deep = rows + 2 * EDGE
    pairs = groups + 1
    body = pl.ds(LANE, cols)

    t = lax.axis_index("sky")
    g = lax.axis_index("visit")
    first = lax.div(t * visits_all, tiles)

    def needs(tile, v):
        start = lax.div(tile * visits_all, tiles)
        return lax.rem(g * visits + v - start + visits_all, visits_all) < DEPTH_MAX

    turn = lax.rem(g - lax.div(first, visits) + groups, groups)
    part = lax.rem(first, visits)
    lo = jnp.where(turn == 0, part, 0)
    hi = jnp.clip(DEPTH_MAX + part - turn * visits, 0, visits)
    twos = lax.div(jnp.maximum(hi - lo, 0) + 1, 2)
    ascend = g >= groups // 2

    def gives(group):
        o = lax.rem(group - lax.div(first, visits) + groups, groups)
        return (o * visits - lax.rem(first, visits)) < DEPTH_MAX

    barrier = pltpu.get_barrier_semaphore()

    @pl.when(t > 0)
    def _():
        pl.semaphore_signal(barrier, inc=1, device_id=(t - 1, g), device_id_type=MESH)

    @pl.when(t < tiles - 1)
    def _():
        pl.semaphore_signal(barrier, inc=1, device_id=(t + 1, g), device_id_type=MESH)

    for d in range(1, groups):
        pl.semaphore_signal(
            barrier, inc=1, device_id=(t, lax.rem(g + d, groups)), device_id_type=MESH
        )

    def img_copy(v):
        return pltpu.make_async_copy(
            img_ref.at[v], buf.at[v, pl.ds(0, rows), body], img_sem.at[v]
        )

    def inv_copy(v):
        return pltpu.make_async_copy(
            inv_ref.at[v], inv.at[v, :, pl.ds(0, cols)], inv_sem.at[v]
        )

    def start_local(v, carry):
        @pl.when(needs(t, v))
        def _():
            img_copy(v).start()
            inv_copy(v).start()

        return carry

    lax.fori_loop(0, visits, start_local, 0)

    def clear(v, carry):
        buf[v, :, :LANE] = jnp.zeros((deep, LANE), jnp.bfloat16)
        buf[v, :, LANE + cols :] = jnp.zeros((deep, width - LANE - cols), jnp.bfloat16)
        inv[v, :, cols:] = jnp.zeros((rows, inv.shape[2] - cols), jnp.bfloat16)

        @pl.when(t == 0)
        def _():
            buf[v, rows + EDGE :, LANE : LANE + cols] = jnp.zeros((EDGE, cols), jnp.bfloat16)

        @pl.when(t == tiles - 1)
        def _():
            buf[v, rows : rows + EDGE, LANE : LANE + cols] = jnp.zeros((EDGE, cols), jnp.bfloat16)

        return carry

    lax.fori_loop(0, visits, clear, 0)

    lower = jnp.where(t > 0, 1, 0)
    upper = jnp.where(t < tiles - 1, 1, 0)
    pl.semaphore_wait(barrier, groups - 1 + lower + upper)

    def halo(n, way, b):
        at = pl.multiple_of(jnp.where(ascend, n, groups - 1 - n) * strip, LANE)
        if way == 0:
            here, there, tile = rows - EDGE, rows + EDGE, lax.rem(t + 1, tiles)
        else:
            here, there, tile = 0, rows, lax.rem(t + tiles - 1, tiles)
        some = pl.ds(b * BATCH, BATCH)
        to = pl.ds(pl.multiple_of(at + LANE, LANE), strip)
        return pltpu.make_async_remote_copy(
            src_ref=img_ref.at[some, pl.ds(here, EDGE), pl.ds(at, strip)],
            dst_ref=buf.at[some, pl.ds(there, EDGE), to],
            send_sem=halo_send.at[n, way, b],
            recv_sem=halo_recv.at[n, way, b],
            device_id=(tile, g),
            device_id_type=MESH,
        )

    def needs_any(tile, b):
        found = needs(tile, b * BATCH)
        for r in range(1, BATCH):
            found = found | needs(tile, b * BATCH + r)
        return found

    def sends(n, b, act):
        @pl.when((t < tiles - 1) & needs_any(t + 1, b))
        def _():
            act(halo(n, 0, b))

        @pl.when((t > 0) & needs_any(t - 1, b))
        def _():
            act(halo(n, 1, b))

    def start_halo(n):
        def one_batch(b, carry):
            sends(n, b, lambda c: c.start())
            return carry

        lax.fori_loop(0, visits // BATCH, one_batch, 0)

    start_halo(0)
    start_halo(1)

    def ready(v, s):
        @pl.when(s == 0)
        def _():
            img_copy(v).wait()

        @pl.when((s < groups) & ((v == lo) | (lax.rem(v, BATCH) == 0)))
        def _():
            b = lax.div(v, BATCH)

            @pl.when(t > 0)
            def _():
                halo(s, 0, b).wait_recv()

            @pl.when(t < tiles - 1)
            def _():
                halo(s, 1, b).wait_recv()

    spot = lax.broadcasted_iota(jnp.int32, (taps, WIN), 1)
    which = lax.broadcasted_iota(jnp.int32, (taps, WIN), 0)

    def placed(ref, wanted):
        picks = jnp.where(wanted == which, 1.0, 0.0).astype(jnp.bfloat16)
        return jnp.dot(ref[...], picks, preferred_element_type=jnp.float32)

    base_ref[0] = placed(row_ref, jnp.where(spot >= WIN - half, spot - WIN, spot) + half)
    base_ref[1] = placed(row_ref, spot - (LANE + EDGE - half))
    base_ref[2] = placed(col_ref, jnp.where(spot == 0, 0, WIN - spot))

    def one_table(k, carry):
        def spread(n, count):
            line = jnp.broadcast_to(base_ref[n, pl.ds(k, 1), :], (count, WIN))
            return pltpu.roll(line, 0, 1, stride=1, stride_axis=0)

        own = spread(0, rows)[:, :LANE]
        above = spread(1, rows)[:, LANE:]
        both = jnp.concatenate([own, above], axis=1).astype(jnp.bfloat16)
        row_tab[k] = both[:, :deep]
        col_tab[k] = spread(2, WIN).astype(jnp.bfloat16)
        return carry

    lax.fori_loop(0, basis, one_table, 0)
    flat[...] = jnp.zeros_like(flat)

    row_ids = t * rows + lax.broadcasted_iota(jnp.int32, (rows, LANE), 0)
    row_coord = (2.0 * row_ids.astype(jnp.float32) + 1.0) / total_rows - 1.0
    row_coord = jnp.concatenate([row_coord] * (WIN // LANE), axis=1)[None]
    lane = lax.broadcasted_iota(jnp.int32, (PAIR, 1, WIN), 2)
    place = lax.broadcasted_iota(jnp.int32, (PAIR, 1, WIN), 0)

    def window(ref, v, at):
        base = pl.multiple_of(lax.div(at, LANE) * LANE, LANE)
        chunk = ref[v, :, pl.ds(base, WIN + LANE)].astype(jnp.float32)
        turn = lax.rem(WIN + LANE - lax.rem(at, LANE), WIN + LANE)
        return pltpu.roll(chunk, turn, 1)[:, :WIN]

    def place_of(s):
        return jnp.where(ascend, s, pairs - 1 - s)

    def row_windows(v, q):
        return [
            window(buf, v, (q * PAIR + j) * step + LANE - half).astype(jnp.bfloat16)
            for j in range(PAIR)
        ]

    def row_half(dst, tall, j):
        made = jnp.dot(
            row_tab[...].reshape(basis * rows, deep), tall[j], preferred_element_type=jnp.float32
        )
        dst[:, j] = made.astype(jnp.bfloat16).reshape(basis, rows, WIN)

    def step_pair(src, v, on, q, dst, v_next, q_next):
        tall = row_windows(v_next, q_next)
        row_half(dst, tall, 0)
        col_ids = (q * PAIR + place) * step + lane
        col_coord = (2.0 * col_ids.astype(jnp.float32) + 1.0) / cols - 1.0
        who = g * visits + v
        shift = shift_ref[who]
        age = lax.rem(who - first + visits_all, visits_all)
        scale = jnp.where((age < depth_ref[0]) & on, 1.0, 0.0)
        matched = jnp.zeros((PAIR, rows, WIN), jnp.float32)
        for k in range(basis):
            if k == basis // 2:
                row_half(dst, tall, 1)
            image = jnp.dot(
                src[k].reshape(PAIR * rows, WIN), col_tab[k], preferred_element_type=jnp.float32
            ).reshape(PAIR, rows, WIN)
            c0 = coef_ref[k, 0, who]
            c1 = coef_ref[k, 1, who]
            c2 = coef_ref[k, 2, who]
            matched = matched + ((c0 + c1 * col_coord) + c2 * row_coord) * image
        weight = jnp.stack([window(inv, v, (q * PAIR + j) * step) for j in range(PAIR)])
        inside = (col_ids >= shift) & (col_ids < shift + cols - DITHER) & (lane < step)
        weight = weight * jnp.where(inside, scale, 0.0)
        acc[...] += weight * matched

    def part_copy(n, d):
        return pltpu.make_async_remote_copy(
            src_ref=outgo.at[n, d - 1],
            dst_ref=income.at[n, d - 1],
            send_sem=part_send.at[n, d - 1],
            recv_sem=part_recv.at[n, d - 1],
            device_id=(t, lax.rem(g + d, groups)),
            device_id_type=MESH,
        )

    total[...] = jnp.zeros_like(total)

    def add_weight(v, carry):
        inv_copy(v).wait()
        who = g * visits + v
        shift = shift_ref[who]
        age = lax.rem(who - first + visits_all, visits_all)
        scale = jnp.where(age < depth_ref[0], 1.0, 0.0)
        for c in range(groups):
            at = c * strip
            ids = at + lax.broadcasted_iota(jnp.int32, (1, strip), 1)
            inside = (ids >= shift) & (ids < shift + cols - DITHER)
            here = inv[v, :, at : at + strip].astype(jnp.float32)
            total[:, at : at + strip] += here * jnp.where(inside, scale, 0.0)
        return carry

    lax.fori_loop(lo, hi, add_weight, 0)

    @pl.when(gives(g))
    def _():
        for d in range(1, groups):
            c = lax.rem(g + d, groups)
            here = total[:, pl.ds(pl.multiple_of(c * strip, LANE), strip)]
            outgo[1, d - 1] = here.astype(jnp.bfloat16)
            part_copy(1, d).start()

    @pl.when(twos > 0)
    def _():
        ready(lo, 0)
        tall = row_windows(lo, place_of(0))
        row_half(pass_a, tall, 0)
        row_half(pass_a, tall, 1)

    def one_pair(s, carry):
        q = place_of(s)
        acc[...] = jnp.zeros_like(acc)

        @pl.when(s + 2 < groups)
        def _():
            start_halo(s + 2)

        def two_visits(i, inner):
            va = lo + 2 * i
            more = va + 1 < hi
            vb = jnp.where(more, va + 1, va)
            final = i == twos - 1
            vn = jnp.where(final, lo, va + 2)
            sn = jnp.where(final, jnp.minimum(s + 1, pairs - 1), s)

            @pl.when(more)
            def _():
                ready(vb, s)

            @pl.when(jnp.logical_not(final) | (s < pairs - 1))
            def _():
                ready(vn, sn)

            step_pair(pass_a, va, True, q, pass_b, vb, q)
            step_pair(pass_b, vb, more, q, pass_a, vn, place_of(sn))
            return inner

        lax.fori_loop(0, twos, two_visits, 0)

        @pl.when(gives(g))
        def _():
            for j in range(PAIR):
                at = (q * PAIR + j) * step
                base = pl.multiple_of(lax.div(at, LANE) * LANE, LANE)
                part = jnp.concatenate([acc[j], jnp.zeros((rows, LANE), jnp.float32)], axis=1)
                flat[:, pl.ds(base, WIN + LANE)] += pltpu.roll(part, lax.rem(at, LANE), 1)

            c = jnp.where(ascend, s - 1, pairs - 1 - s)

            @pl.when((s > 0) & (c != g))
            def _():
                d = lax.rem(c - g + groups, groups)
                here = flat[:, pl.ds(pl.multiple_of(c * strip, LANE), strip)]
                outgo[0, d - 1] = here.astype(jnp.bfloat16)
                part_copy(0, d).start()

        return carry

    lax.fori_loop(0, pairs, one_pair, 0)

    mine = pl.ds(pl.multiple_of(g * strip, LANE), strip)
    for d in range(1, groups):
        @pl.when(gives(lax.rem(g - d + groups, groups)))
        def _():
            for n, held in enumerate((flat, total)):
                part_copy(n, d).wait_recv()
                held[:, mine] += income[n, d - 1].astype(jnp.float32)

    out_ref[...] = flat[:, mine] / (1.0 + total[:, mine])

    @pl.when(gives(g))
    def _():
        for n in range(2):
            for d in range(1, groups):
                part_copy(n, d).wait_send()

    def end_halo(n, carry):
        def one_batch(b, inner):
            sends(n, b, lambda c: c.wait_send())
            return inner

        lax.fori_loop(0, visits // BATCH, one_batch, 0)
        return carry

    lax.fori_loop(0, groups, end_halo, 0)


def local(images, inv_var, row_taps, col_taps, coeffs, dithers, depths):
    visits, rows, cols = images.shape
    basis, taps = row_taps.shape
    tiles = lax.axis_size("sky")
    groups = lax.axis_size("visit")
    step = WIN - taps + 1
    pairs = groups + 1
    strip = cols // groups
    room = cols + WIN
    deep = rows + 2 * EDGE
    sizes = (tiles, groups, step)

    def run(*refs):
        kernel(sizes, *refs)

    smem = pl.BlockSpec(memory_space=pltpu.SMEM)
    vmem = pl.BlockSpec(memory_space=pltpu.VMEM)
    hbm = pl.BlockSpec(memory_space=pl.ANY)
    dma = pltpu.SemaphoreType.DMA
    flops = 2 * visits * pairs * PAIR * 2 * basis * rows * WIN * WIN
    return pl.pallas_call(
        run,
        out_shape=jax.ShapeDtypeStruct((rows, strip), jnp.float32),
        in_specs=[smem, smem, smem, vmem, vmem, hbm, hbm],
        out_specs=vmem,
        scratch_shapes=[
            pltpu.VMEM((visits, deep, LANE + cols + WIN), jnp.bfloat16),
            pltpu.VMEM((visits, rows, room), jnp.bfloat16),
            pltpu.VMEM((3, basis, WIN), jnp.float32),
            pltpu.VMEM((basis, rows, deep), jnp.bfloat16),
            pltpu.VMEM((basis, WIN, WIN), jnp.bfloat16),
            pltpu.VMEM((basis, PAIR, rows, WIN), jnp.bfloat16),
            pltpu.VMEM((basis, PAIR, rows, WIN), jnp.bfloat16),
            pltpu.VMEM((PAIR, rows, WIN), jnp.float32),
            pltpu.VMEM((rows, room), jnp.float32),
            pltpu.VMEM((rows, cols), jnp.float32),
            pltpu.VMEM((2, groups - 1, rows, strip), jnp.bfloat16),
            pltpu.VMEM((2, groups - 1, rows, strip), jnp.bfloat16),
            dma((visits,)),
            dma((visits,)),
            dma((groups, 2, visits // BATCH)),
            dma((groups, 2, visits // BATCH)),
            dma((2, groups - 1)),
            dma((2, groups - 1)),
        ],
        compiler_params=pltpu.CompilerParams(
            vmem_limit_bytes=52 * 1024 * 1024, collective_id=0, has_side_effects=True
        ),
        cost_estimate=pl.CostEstimate(
            flops=flops, bytes_accessed=4 * visits * rows * cols, transcendentals=0
        ),
    )(jnp.transpose(coeffs, (1, 2, 0)), dithers, depths, row_taps, col_taps, images, inv_var)


def solution(mesh):
    placed = (P("visit", "sky", None), P("visit", "sky", None), P(), P(), P(), P(), P("sky"))
    return jax.shard_map(
        local, mesh=mesh, in_specs=placed, out_specs=P("sky", "visit"), check_vma=False
    )
```

```python
import jax
import jax.numpy as jnp
from jax import lax
from jax.experimental import pallas as pl
from jax.experimental.pallas import tpu as pltpu
from jax.sharding import PartitionSpec as P

DITHER = 256
DEPTH_MAX = 16
WIN = 256
PAIR = 2
LANE = 128
EDGE = 32
BATCH = 4
MESH = pl.DeviceIdType.MESH


def kernel(
    sizes,
    coef_ref, shift_ref, depth_ref, row_ref, col_ref, img_ref, inv_ref,
    out_ref,
    buf, inv, base_ref, row_tab, col_tab, pass_a, pass_b, acc, flat, total, outgo, income,
    img_sem, inv_sem, halo_send, halo_recv, part_send, part_recv,
):
    tiles, groups, step = sizes
    visits, rows, cols = img_ref.shape
    basis, taps = row_ref.shape
    half = taps // 2
    visits_all = visits * groups
    total_rows = rows * tiles
    strip = cols // groups
    width = buf.shape[2]
    deep = rows + 2 * EDGE
    pairs = groups + 1
    body = pl.ds(LANE, cols)

    t = lax.axis_index("sky")
    g = lax.axis_index("visit")
    first = lax.div(t * visits_all, tiles)

    def needs(tile, v):
        start = lax.div(tile * visits_all, tiles)
        return lax.rem(g * visits + v - start + visits_all, visits_all) < DEPTH_MAX

    turn = lax.rem(g - lax.div(first, visits) + groups, groups)
    part = lax.rem(first, visits)
    lo = jnp.where(turn == 0, part, 0)
    hi = jnp.clip(DEPTH_MAX + part - turn * visits, 0, visits)
    twos = lax.div(jnp.maximum(hi - lo, 0) + 1, 2)
    ascend = g >= groups // 2

    def gives(group):
        o = lax.rem(group - lax.div(first, visits) + groups, groups)
        return (o * visits - lax.rem(first, visits)) < DEPTH_MAX

    barrier = pltpu.get_barrier_semaphore()

    @pl.when(t > 0)
    def _():
        pl.semaphore_signal(barrier, inc=1, device_id=(t - 1, g), device_id_type=MESH)

    @pl.when(t < tiles - 1)
    def _():
        pl.semaphore_signal(barrier, inc=1, device_id=(t + 1, g), device_id_type=MESH)

    for d in range(1, groups):
        pl.semaphore_signal(
            barrier, inc=1, device_id=(t, lax.rem(g + d, groups)), device_id_type=MESH
        )

    def img_copy(v):
        return pltpu.make_async_copy(
            img_ref.at[v], buf.at[v, pl.ds(0, rows), body], img_sem.at[v]
        )

    def inv_copy(v):
        return pltpu.make_async_copy(
            inv_ref.at[v], inv.at[v, :, pl.ds(0, cols)], inv_sem.at[v]
        )

    def start_local(v, carry):
        @pl.when(needs(t, v))
        def _():
            img_copy(v).start()
            inv_copy(v).start()

        return carry

    lax.fori_loop(0, visits, start_local, 0)

    def clear(v, carry):
        buf[v, :, :LANE] = jnp.zeros((deep, LANE), jnp.bfloat16)
        buf[v, :, LANE + cols :] = jnp.zeros((deep, width - LANE - cols), jnp.bfloat16)
        inv[v, :, cols:] = jnp.zeros((rows, inv.shape[2] - cols), jnp.bfloat16)

        @pl.when(t == 0)
        def _():
            buf[v, rows + EDGE :, LANE : LANE + cols] = jnp.zeros((EDGE, cols), jnp.bfloat16)

        @pl.when(t == tiles - 1)
        def _():
            buf[v, rows : rows + EDGE, LANE : LANE + cols] = jnp.zeros((EDGE, cols), jnp.bfloat16)

        return carry

    lax.fori_loop(0, visits, clear, 0)

    lower = jnp.where(t > 0, 1, 0)
    upper = jnp.where(t < tiles - 1, 1, 0)
    pl.semaphore_wait(barrier, groups - 1 + lower + upper)

    def halo(n, way, b):
        at = pl.multiple_of(jnp.where(ascend, n, groups - 1 - n) * strip, LANE)
        if way == 0:
            here, there, tile = rows - EDGE, rows + EDGE, lax.rem(t + 1, tiles)
        else:
            here, there, tile = 0, rows, lax.rem(t + tiles - 1, tiles)
        some = pl.ds(b * BATCH, BATCH)
        to = pl.ds(pl.multiple_of(at + LANE, LANE), strip)
        return pltpu.make_async_remote_copy(
            src_ref=img_ref.at[some, pl.ds(here, EDGE), pl.ds(at, strip)],
            dst_ref=buf.at[some, pl.ds(there, EDGE), to],
            send_sem=halo_send.at[n, way, b],
            recv_sem=halo_recv.at[n, way, b],
            device_id=(tile, g),
            device_id_type=MESH,
        )

    def needs_any(tile, b):
        found = needs(tile, b * BATCH)
        for r in range(1, BATCH):
            found = found | needs(tile, b * BATCH + r)
        return found

    def sends(n, b, act):
        @pl.when((t < tiles - 1) & needs_any(t + 1, b))
        def _():
            act(halo(n, 0, b))

        @pl.when((t > 0) & needs_any(t - 1, b))
        def _():
            act(halo(n, 1, b))

    def start_halo(n):
        def one_batch(b, carry):
            sends(n, b, lambda c: c.start())
            return carry

        lax.fori_loop(0, visits // BATCH, one_batch, 0)

    start_halo(0)

    def ready(v, s):
        @pl.when(s == 0)
        def _():
            img_copy(v).wait()

        @pl.when((s < groups) & ((v == lo) | (lax.rem(v, BATCH) == 0)))
        def _():
            b = lax.div(v, BATCH)

            @pl.when(t > 0)
            def _():
                halo(s, 0, b).wait_recv()

            @pl.when(t < tiles - 1)
            def _():
                halo(s, 1, b).wait_recv()

    spot = lax.broadcasted_iota(jnp.int32, (taps, WIN), 1)
    which = lax.broadcasted_iota(jnp.int32, (taps, WIN), 0)

    def placed(ref, wanted):
        picks = jnp.where(wanted == which, 1.0, 0.0).astype(jnp.bfloat16)
        return jnp.dot(ref[...], picks, preferred_element_type=jnp.float32)

    base_ref[0] = placed(row_ref, jnp.where(spot >= WIN - half, spot - WIN, spot) + half)
    base_ref[1] = placed(row_ref, spot - (LANE + EDGE - half))
    base_ref[2] = placed(col_ref, jnp.where(spot == 0, 0, WIN - spot))

    def one_table(k, carry):
        def spread(n, count):
            line = jnp.broadcast_to(base_ref[n, pl.ds(k, 1), :], (count, WIN))
            return pltpu.roll(line, 0, 1, stride=1, stride_axis=0)

        own = spread(0, rows)[:, :LANE]
        above = spread(1, rows)[:, LANE:]
        both = jnp.concatenate([own, above], axis=1).astype(jnp.bfloat16)
        row_tab[k] = both[:, :deep]
        col_tab[k] = spread(2, WIN).astype(jnp.bfloat16)
        return carry

    lax.fori_loop(0, basis, one_table, 0)
    flat[...] = jnp.zeros_like(flat)

    row_ids = t * rows + lax.broadcasted_iota(jnp.int32, (rows, LANE), 0)
    row_coord = (2.0 * row_ids.astype(jnp.float32) + 1.0) / total_rows - 1.0
    row_coord = jnp.concatenate([row_coord] * (WIN // LANE), axis=1)[None]
    lane = lax.broadcasted_iota(jnp.int32, (PAIR, 1, WIN), 2)
    place = lax.broadcasted_iota(jnp.int32, (PAIR, 1, WIN), 0)

    def window(ref, v, at):
        base = pl.multiple_of(lax.div(at, LANE) * LANE, LANE)
        chunk = ref[v, :, pl.ds(base, WIN + LANE)].astype(jnp.float32)
        turn = lax.rem(WIN + LANE - lax.rem(at, LANE), WIN + LANE)
        return pltpu.roll(chunk, turn, 1)[:, :WIN]

    def place_of(s):
        return jnp.where(ascend, s, pairs - 1 - s)

    def row_windows(v, q):
        return [
            window(buf, v, (q * PAIR + j) * step + LANE - half).astype(jnp.bfloat16)
            for j in range(PAIR)
        ]

    def row_half(dst, tall, j):
        made = jnp.dot(
            row_tab[...].reshape(basis * rows, deep), tall[j], preferred_element_type=jnp.float32
        )
        dst[:, j] = made.astype(jnp.bfloat16).reshape(basis, rows, WIN)

    def step_pair(src, v, on, q, dst, v_next, q_next):
        tall = row_windows(v_next, q_next)
        row_half(dst, tall, 0)
        col_ids = (q * PAIR + place) * step + lane
        col_coord = (2.0 * col_ids.astype(jnp.float32) + 1.0) / cols - 1.0
        who = g * visits + v
        shift = shift_ref[who]
        age = lax.rem(who - first + visits_all, visits_all)
        scale = jnp.where((age < depth_ref[0]) & on, 1.0, 0.0)
        matched = jnp.zeros((PAIR, rows, WIN), jnp.float32)
        for k in range(basis):
            if k == basis // 2:
                row_half(dst, tall, 1)
            image = jnp.dot(
                src[k].reshape(PAIR * rows, WIN), col_tab[k], preferred_element_type=jnp.float32
            ).reshape(PAIR, rows, WIN)
            c0 = coef_ref[k, 0, who]
            c1 = coef_ref[k, 1, who]
            c2 = coef_ref[k, 2, who]
            matched = matched + ((c0 + c1 * col_coord) + c2 * row_coord) * image
        weight = jnp.stack([window(inv, v, (q * PAIR + j) * step) for j in range(PAIR)])
        inside = (col_ids >= shift) & (col_ids < shift + cols - DITHER) & (lane < step)
        weight = weight * jnp.where(inside, scale, 0.0)
        acc[...] += weight * matched

    def part_copy(n, d):
        return pltpu.make_async_remote_copy(
            src_ref=outgo.at[n, d - 1],
            dst_ref=income.at[n, d - 1],
            send_sem=part_send.at[n, d - 1],
            recv_sem=part_recv.at[n, d - 1],
            device_id=(t, lax.rem(g + d, groups)),
            device_id_type=MESH,
        )

    total[...] = jnp.zeros_like(total)

    def add_weight(v, carry):
        inv_copy(v).wait()
        who = g * visits + v
        shift = shift_ref[who]
        age = lax.rem(who - first + visits_all, visits_all)
        scale = jnp.where(age < depth_ref[0], 1.0, 0.0)
        for c in range(groups):
            at = c * strip
            ids = at + lax.broadcasted_iota(jnp.int32, (1, strip), 1)
            inside = (ids >= shift) & (ids < shift + cols - DITHER)
            here = inv[v, :, at : at + strip].astype(jnp.float32)
            total[:, at : at + strip] += here * jnp.where(inside, scale, 0.0)
        return carry

    lax.fori_loop(lo, hi, add_weight, 0)
    start_halo(1)

    @pl.when(gives(g))
    def _():
        for d in range(1, groups):
            c = lax.rem(g + d, groups)
            here = total[:, pl.ds(pl.multiple_of(c * strip, LANE), strip)]
            outgo[1, d - 1] = here.astype(jnp.bfloat16)
            part_copy(1, d).start()

    @pl.when(twos > 0)
    def _():
        ready(lo, 0)
        tall = row_windows(lo, place_of(0))
        row_half(pass_a, tall, 0)
        row_half(pass_a, tall, 1)

    def one_pair(s, carry):
        q = place_of(s)
        acc[...] = jnp.zeros_like(acc)

        @pl.when(s + 2 < groups)
        def _():
            start_halo(s + 2)

        def two_visits(i, inner):
            va = lo + 2 * i
            more = va + 1 < hi
            vb = jnp.where(more, va + 1, va)
            final = i == twos - 1
            vn = jnp.where(final, lo, va + 2)
            sn = jnp.where(final, jnp.minimum(s + 1, pairs - 1), s)

            @pl.when(more)
            def _():
                ready(vb, s)

            @pl.when(jnp.logical_not(final) | (s < pairs - 1))
            def _():
                ready(vn, sn)

            step_pair(pass_a, va, True, q, pass_b, vb, q)
            step_pair(pass_b, vb, more, q, pass_a, vn, place_of(sn))
            return inner

        lax.fori_loop(0, twos, two_visits, 0)

        @pl.when(gives(g))
        def _():
            for j in range(PAIR):
                at = (q * PAIR + j) * step
                base = pl.multiple_of(lax.div(at, LANE) * LANE, LANE)
                part = jnp.concatenate([acc[j], jnp.zeros((rows, LANE), jnp.float32)], axis=1)
                flat[:, pl.ds(base, WIN + LANE)] += pltpu.roll(part, lax.rem(at, LANE), 1)

            c = jnp.where(ascend, s - 1, pairs - 1 - s)

            @pl.when((s > 0) & (c != g))
            def _():
                d = lax.rem(c - g + groups, groups)
                here = flat[:, pl.ds(pl.multiple_of(c * strip, LANE), strip)]
                outgo[0, d - 1] = here.astype(jnp.bfloat16)
                part_copy(0, d).start()

        return carry

    lax.fori_loop(0, pairs, one_pair, 0)

    mine = pl.ds(pl.multiple_of(g * strip, LANE), strip)
    for d in range(1, groups):
        @pl.when(gives(lax.rem(g - d + groups, groups)))
        def _():
            for n, held in enumerate((flat, total)):
                part_copy(n, d).wait_recv()
                held[:, mine] += income[n, d - 1].astype(jnp.float32)

    out_ref[...] = flat[:, mine] / (1.0 + total[:, mine])

    @pl.when(gives(g))
    def _():
        for n in range(2):
            for d in range(1, groups):
                part_copy(n, d).wait_send()

    def end_halo(n, carry):
        def one_batch(b, inner):
            sends(n, b, lambda c: c.wait_send())
            return inner

        lax.fori_loop(0, visits // BATCH, one_batch, 0)
        return carry

    lax.fori_loop(0, groups, end_halo, 0)


def local(images, inv_var, row_taps, col_taps, coeffs, dithers, depths):
    visits, rows, cols = images.shape
    basis, taps = row_taps.shape
    tiles = lax.axis_size("sky")
    groups = lax.axis_size("visit")
    step = WIN - taps + 1
    pairs = groups + 1
    strip = cols // groups
    room = cols + WIN
    deep = rows + 2 * EDGE
    sizes = (tiles, groups, step)

    def run(*refs):
        kernel(sizes, *refs)

    smem = pl.BlockSpec(memory_space=pltpu.SMEM)
    vmem = pl.BlockSpec(memory_space=pltpu.VMEM)
    hbm = pl.BlockSpec(memory_space=pl.ANY)
    dma = pltpu.SemaphoreType.DMA
    flops = 2 * visits * pairs * PAIR * 2 * basis * rows * WIN * WIN
    return pl.pallas_call(
        run,
        out_shape=jax.ShapeDtypeStruct((rows, strip), jnp.float32),
        in_specs=[smem, smem, smem, vmem, vmem, hbm, hbm],
        out_specs=vmem,
        scratch_shapes=[
            pltpu.VMEM((visits, deep, LANE + cols + WIN), jnp.bfloat16),
            pltpu.VMEM((visits, rows, room), jnp.bfloat16),
            pltpu.VMEM((3, basis, WIN), jnp.float32),
            pltpu.VMEM((basis, rows, deep), jnp.bfloat16),
            pltpu.VMEM((basis, WIN, WIN), jnp.bfloat16),
            pltpu.VMEM((basis, PAIR, rows, WIN), jnp.bfloat16),
            pltpu.VMEM((basis, PAIR, rows, WIN), jnp.bfloat16),
            pltpu.VMEM((PAIR, rows, WIN), jnp.float32),
            pltpu.VMEM((rows, room), jnp.float32),
            pltpu.VMEM((rows, cols), jnp.float32),
            pltpu.VMEM((2, groups - 1, rows, strip), jnp.bfloat16),
            pltpu.VMEM((2, groups - 1, rows, strip), jnp.bfloat16),
            dma((visits,)),
            dma((visits,)),
            dma((groups, 2, visits // BATCH)),
            dma((groups, 2, visits // BATCH)),
            dma((2, groups - 1)),
            dma((2, groups - 1)),
        ],
        compiler_params=pltpu.CompilerParams(
            vmem_limit_bytes=57 * 1024 * 1024, collective_id=0, has_side_effects=True
        ),
        cost_estimate=pl.CostEstimate(
            flops=flops, bytes_accessed=4 * visits * rows * cols, transcendentals=0
        ),
    )(jnp.transpose(coeffs, (1, 2, 0)), dithers, depths, row_taps, col_taps, images, inv_var)


def solution(mesh):
    placed = (P("visit", "sky", None), P("visit", "sky", None), P(), P(), P(), P(), P("sky"))
    return jax.shard_map(
        local, mesh=mesh, in_specs=placed, out_specs=P("sky", "visit"), check_vma=False
    )
```
